32 devices in a mesh: batch: 8 (over z, y), seq: 4 (over x, core).
Axes of the slice: x: 2, y: 2, z: 4, core: 2. Of those that a mesh axis runs over, the one named last changes fastest.
Arguments:
- tokens: bfloat16 [16, 2048, 768], P('batch', 'seq'), may hold values from -6 to 6
- lengths: int32 [16], P('batch'), may hold values from 1024 to 2048, as said below
- picks: int32 [16, 256], P('batch', 'seq'), may hold values from 0 to 2047, as said below
- w_router: bfloat16 [768], replicated, may hold values from -0.21875 to 0.21875
- gain_attn: float32 [768], replicated, may hold values from 0.1 to 1.9
- gain_mlp: float32 [768], replicated, may hold values from 0.1 to 1.9
- w_query: bfloat16 [768, 768], replicated, may hold values from -0.21875 to 0.21875
- w_key: bfloat16 [768, 768], replicated, may hold values from -0.21875 to 0.21875
- w_value: bfloat16 [768, 768], replicated, may hold values from -0.21875 to 0.21875
- w_out: bfloat16 [768, 768], replicated, may hold values from -1.75 to 1.75
- w_up: bfloat16 [768, 3072], P(None, 'seq'), may hold values from -0.21875 to 0.21875
- w_down: bfloat16 [3072, 768], P('seq'), may hold values from -0.21875 to 0.21875
- cotangent: bfloat16 [16, 2048, 768], P('batch', 'seq'), may hold values from -6 to 6
Outputs:
- output: bfloat16 [16, 2048, 768], P('batch', 'seq')
- grad_tokens: bfloat16 [16, 2048, 768], P('batch', 'seq')
- grad_router: float32 [768], replicated
- grad_gain_attn: float32 [768], replicated
- grad_gain_mlp: float32 [768], replicated
- grad_query: float32 [768, 768], replicated
- grad_key: float32 [768, 768], replicated
- grad_value: float32 [768, 768], replicated
- grad_out: float32 [768, 768], replicated
- grad_up: float32 [768, 3072], P(None, 'seq')
- grad_down: float32 [3072, 768], P('seq')
The draws below stay inside these ranges and needn't reach their ends.
Inputs may be any that keep to these rules, and one draw needn't show every extreme that they name: `lengths`: a multiple of 8; among the 2 sequences of each index of batch at least one has length 2048. `picks`: each row rises strictly; its first lengths // 8 entries are positions below the sequence's length, the others positions at or beyond it.
All inputs are finite; a program needn't handle non-finite values.
Results may differ from the reference program's by a relative error of at most 0.012.
The reference program's roundings to bfloat16 on the way count: a program that leaves them out, or rounds other values in their place, can miss the bound.
Values may be sent and summed in bfloat16 or wider, within the bound.
No kernel may reach another device: no remote copies, remote signals or barrier semaphores. Data moves between devices by JAX's collectives and lax.ppermute only.
A program may use at most 128 MiB of HBM per device.

```python
import jax
import jax.numpy as jnp
from jax import lax

D = 768
NH = 12
HD = 64
FF = 3072
SEQ_LEN = 2048
SEQS = 2
SLOTS = 256
NSEQ = 16


def choose_slots(key):
    length_key, full_key, pick_key = jax.random.split(key, 3)
    groups = NSEQ // SEQS
    drawn = jax.random.randint(length_key, (groups, SEQS), SEQ_LEN // 16, SEQ_LEN // 8 + 1) * 8
    full = jax.random.randint(full_key, (groups, 1), 0, SEQS)
    lengths = jnp.where(jnp.arange(SEQS)[None, :] == full, SEQ_LEN, drawn).reshape(NSEQ).astype(jnp.int32)

    def one_row(row_key, length):
        places = jnp.arange(SEQ_LEN)
        shuffled = jax.random.permutation(row_key, SEQ_LEN)
        ranked = jnp.where(places < length, shuffled, shuffled + SEQ_LEN)
        order = jnp.argsort(ranked)
        count = length // 8
        taken = jnp.zeros(SEQ_LEN, jnp.int32).at[order].set((places < count).astype(jnp.int32))
        taken = jnp.where(places >= SEQ_LEN - (SLOTS - count), 1, taken)
        sorted_places = jnp.argsort(jnp.where(taken > 0, places, places + SEQ_LEN))
        return sorted_places[:SLOTS].astype(jnp.int32)
    picks = jax.vmap(one_row)(jax.random.split(pick_key, NSEQ), lengths)
    return (lengths, picks)


def draw_lengths(key, part):
    lengths, picks = choose_slots(key)
    return lengths


def draw_picks(key, part):
    lengths, picks = choose_slots(key)
    return picks


def block_scale(rng, shape, cuts, low, top_value):
    level, own = 1.0, jax.random.fold_in(rng, 6)
    for dim, parts in cuts:
        heights = jnp.exp(jax.random.uniform(jax.random.fold_in(own, dim), (parts,), jnp.float32, low / len(cuts), top_value / len(cuts)))
        level = level * jnp.repeat(heights, shape[dim] // parts).reshape([-1 if axis == dim else 1 for axis in range(len(shape))])
    return level


def bell_draw(stream_key, shape, spread, most, pieces=(), held_as=jnp.bfloat16):
    result = spread * jax.random.normal(stream_key, shape, jnp.float32)
    if pieces:
        result = result * block_scale(stream_key, shape, pieces, -0.22, 0.18)
    return jnp.clip(result, -most, most).astype(held_as)


def setup_inputs(seed: int = 0) -> dict:
    seeds = jax.random.split(jax.random.key(seed), 14)
    tokens = bell_draw(seeds[0], (NSEQ, SEQ_LEN, D), 1.0, 6.0, ((0, 8), (1, 4)))
    lengths = draw_lengths(jax.random.fold_in(seeds[13], 71), 0)
    picks = draw_picks(jax.random.fold_in(seeds[13], 71), 0)
    w_router = bell_draw(seeds[3], (D,), D ** -0.5, 0.21875)
    gain_attn = jnp.clip(1.0 + 0.18 * jax.random.normal(seeds[4], (D,), jnp.float32), 0.1, 1.9)
    gain_mlp = jnp.clip(1.0 + 0.18 * jax.random.normal(seeds[5], (D,), jnp.float32), 0.1, 1.9)
    w_query = bell_draw(seeds[6], (D, D), D ** -0.5, 0.21875)
    w_key = bell_draw(seeds[7], (D, D), D ** -0.5, 0.21875)
    w_value = bell_draw(seeds[8], (D, D), D ** -0.5, 0.21875)
    w_out = bell_draw(seeds[9], (D, D), (D // 64) ** -0.5, 1.75)
    w_up = bell_draw(seeds[10], (D, FF), D ** -0.5, 0.21875, ((1, 4),))
    w_down = bell_draw(seeds[11], (FF, D), (FF // 4) ** -0.5, 0.21875, ((0, 4),))
    cotangent = bell_draw(seeds[12], (NSEQ, SEQ_LEN, D), 1.0, 6.0, ((0, 8), (1, 4)))
    return dict(tokens=tokens, lengths=lengths, picks=picks, w_router=w_router, gain_attn=gain_attn, gain_mlp=gain_mlp, w_query=w_query, w_key=w_key, w_value=w_value, w_out=w_out, w_up=w_up, w_down=w_down, cotangent=cotangent)


@jax.custom_vjp
def low(v):
    return lax.optimization_barrier(v.astype(jnp.bfloat16)).astype(jnp.float32)

@jax.custom_vjp
def low_back(v):
    return v

def low_keep(v):
    return (low(v), None)

def low_pass(kept, grad):
    return (grad,)

def back_keep(v):
    return (v, None)

def back_low(kept, grad):
    return (low(grad),)
low.defvjp(low_keep, low_pass)
low_back.defvjp(back_keep, back_low)

def norm_scale(values, gain):
    return values * lax.rsqrt(lax.optimization_barrier(jnp.mean(values * values, axis=-1, keepdims=True)) + 1e-06) * gain

def one_sequence(weights, row, picked, length):
    w_router, gain_attn, gain_mlp, w_query, w_key, w_value, w_out, w_up, w_down = weights
    highest = lax.Precision.HIGHEST
    slots = picked.shape[0]
    chosen = low_back(row[picked])
    count = length // 8
    order = jnp.arange(slots)
    valid = (order < count).astype(row.dtype)
    rate = jax.nn.sigmoid(jnp.dot(chosen, w_router, precision=highest))
    normed = low(norm_scale(chosen, gain_attn))
    query = low_back(low(jnp.dot(normed, w_query, precision=highest))).reshape(slots, NH, HD)
    keys = low_back(low(jnp.dot(normed, w_key, precision=highest))).reshape(slots, NH, HD)
    values = low_back(low(jnp.dot(normed, w_value, precision=highest))).reshape(slots, NH, HD)
    logits = low_back(jnp.einsum('ihd,jhd->hij', query, keys, precision=highest) * HD ** (-0.5))
    allowed = (order[None, :] <= order[:, None]) & (order[None, :] < count)
    logits = jnp.where(allowed[None], logits, -1e+30)
    highest_logit = lax.optimization_barrier(jnp.max(logits, axis=-1, keepdims=True))
    expd = jnp.exp(logits - highest_logit)
    probs = expd / lax.optimization_barrier(jnp.sum(expd, axis=-1, keepdims=True))
    mixed = jnp.einsum('hij,jhd->ihd', low(probs), values, precision=highest).reshape(slots, NH * HD)
    mixed = low_back(low(mixed))
    attended = low_back(jnp.dot(mixed, w_out, precision=highest))
    hidden = chosen + attended
    normed_mlp = low(norm_scale(hidden, gain_mlp))
    up_proj = low_back(jnp.dot(normed_mlp, w_up, precision=highest))
    activated = low(jax.nn.gelu(up_proj))
    moved = low_back(jnp.dot(activated, w_down, precision=highest))
    update = low((rate * valid)[:, None] * (attended + moved))
    return row.at[picked].add(update)

def reference(tokens, lengths, picks, w_router, gain_attn, gain_mlp, w_query, w_key, w_value, w_out, w_up, w_down, cotangent):
    inputs = tokens.astype(jnp.float32)
    weights = (w_router.astype(jnp.float32), gain_attn.astype(jnp.float32), gain_mlp.astype(jnp.float32), w_query.astype(jnp.float32), w_key.astype(jnp.float32), w_value.astype(jnp.float32), w_out.astype(jnp.float32), w_up.astype(jnp.float32), w_down.astype(jnp.float32))

    def forward(inputs, weights):

        def step(item):
            row, picked, length = item
            return one_sequence(weights, row, picked, length)
        return lax.map(jax.checkpoint(step), (inputs, picks, lengths))
    output, backward = jax.vjp(forward, inputs, weights)
    grad_inputs, grad_weights = backward(cotangent.astype(jnp.float32))
    return (output.astype(jnp.bfloat16), grad_inputs.astype(jnp.bfloat16), grad_weights[0], grad_weights[1], grad_weights[2], grad_weights[3], grad_weights[4], grad_weights[5], grad_weights[6], grad_weights[7], grad_weights[8])
```

```python
import functools

import jax
import jax.numpy as jnp
from jax import lax
from jax.experimental import pallas as pl
from jax.experimental.pallas import tpu as pltpu
from jax.sharding import PartitionSpec as P

NH = 12
EPS = 1e-06
F32 = jnp.float32
BF16 = jnp.bfloat16
VMEM = pl.BlockSpec(memory_space=pltpu.VMEM)
SMEM = pl.BlockSpec(memory_space=pltpu.SMEM)


def mm(a, b):
    return jnp.dot(a, b, preferred_element_type=F32)


def mm_nt(a, b):
    return lax.dot_general(a, b, (((1,), (1,)), ((), ())), preferred_element_type=F32)


def mm_tn(a, b):
    return lax.dot_general(a, b, (((0,), (0,)), ((), ())), preferred_element_type=F32)


def call(kernel, ins, outs, specs=None, scratch=(), vmem=40, flops=0):
    shapes = tuple(jax.ShapeDtypeStruct(shape, dtype) for shape, dtype in outs)
    moved = sum(v.size * v.dtype.itemsize for v in list(ins) + list(shapes))
    return pl.pallas_call(
        kernel,
        out_shape=shapes,
        in_specs=specs or [VMEM] * len(ins),
        out_specs=tuple(VMEM for _ in shapes),
        scratch_shapes=list(scratch),
        cost_estimate=pl.CostEstimate(flops=flops, bytes_accessed=moved, transcendentals=0),
        compiler_params=pltpu.CompilerParams(vmem_limit_bytes=vmem * 1024 * 1024),
    )(*ins)


def select_kernel(meta, p0, p1, p2, p3, rows, own, other, hot):
    core = meta[1]
    length = rows.shape[1]
    local = p0.shape[1]
    base = meta[0] * length
    down = lax.broadcasted_iota(jnp.int32, (local, local), 0)
    along = lax.broadcasted_iota(jnp.int32, (local, local), 1)
    places = lax.broadcasted_iota(jnp.int32, (local, length), 1)
    for seq, out in ((1 - core, other), (core, own)):
        for k, part in enumerate((p0, p1, p2, p3)):
            row = part[pl.ds(seq, 1), :]
            column = jnp.sum(jnp.where(down == along, row, 0), axis=1, keepdims=True)
            at = pl.multiple_of(meta[4 + k] * local, local)
            hot[pl.ds(at, local), :] = jnp.where(column - base == places, 1.0, 0.0).astype(BF16)
        out[...] = mm(hot[...], rows[seq]).astype(BF16)


def place_kernel(meta, picks, rows, own, other, out):
    core = meta[1]
    length = rows.shape[1]
    slots = picks.shape[1]
    base = meta[0] * length
    places = lax.broadcasted_iota(jnp.int32, (length, slots), 0) + base
    for seq, update in ((core, own), (1 - core, other)):
        hot = jnp.where(picks[pl.ds(seq, 1), :] == places, 1.0, 0.0).astype(BF16)
        out[seq] = (rows[seq].astype(F32) + mm(hot, update[...])).astype(BF16)


def attend_kernel(
    meta, here, there, w_router, gain_attn, gain_mlp, w_query, w_key, w_value, w_out,
    chosen_out, normed_out, query_out, key_out, value_out, probs_out, mixed_out, attended_out,
    normed_mlp_out, rate_out,
):
    count = meta[2]
    slots, width = here.shape
    chosen = here[...].astype(F32) + there[...].astype(F32)
    chosen_out[...] = chosen.astype(BF16)
    score = jnp.sum(chosen * w_router[...].astype(F32), axis=-1, keepdims=True)
    rate = jax.nn.sigmoid(score)
    valid = lax.broadcasted_iota(jnp.int32, (slots, 1), 0) < count
    rate_out[...] = jnp.broadcast_to(jnp.where(valid, rate, 0.0), rate_out.shape)
    scale = lax.rsqrt(jnp.mean(chosen * chosen, axis=-1, keepdims=True) + EPS)
    normed = (chosen * scale * gain_attn[...]).astype(BF16)
    normed_out[...] = normed
    query_out[...] = mm(normed, w_query[...]).astype(BF16)
    key_out[...] = mm(normed, w_key[...]).astype(BF16)
    value_out[...] = mm(normed, w_value[...]).astype(BF16)
    head = width // NH
    pair = 2 * head
    i = lax.broadcasted_iota(jnp.int32, (slots, slots), 0)
    j = lax.broadcasted_iota(jnp.int32, (slots, slots), 1)
    allowed = (j <= i) & (j < count)
    first = lax.broadcasted_iota(jnp.int32, (slots, pair), 1) < head
    for p in range(NH // 2):
        cols = slice(p * pair, (p + 1) * pair)
        query = query_out[:, cols]
        keys = key_out[:, cols]
        values = value_out[:, cols]
        halves = []
        for h in range(2):
            mine = first if h == 0 else ~first
            logits = mm_nt(jnp.where(mine, query, jnp.zeros_like(query)), keys) * (head ** -0.5)
            logits = jnp.where(allowed, logits, -1e30)
            expd = jnp.exp(logits - jnp.max(logits, axis=-1, keepdims=True))
            probs = expd / jnp.sum(expd, axis=-1, keepdims=True)
            probs_out[2 * p + h] = probs
            halves.append(mm(probs.astype(BF16), values))
        mixed_out[:, cols] = jnp.where(first, halves[0], halves[1]).astype(BF16)
    attended = mm(mixed_out[...], w_out[...])
    attended_out[...] = attended
    hidden = chosen + attended
    scale = lax.rsqrt(jnp.mean(hidden * hidden, axis=-1, keepdims=True) + EPS)
    normed_mlp_out[...] = (hidden * scale * gain_mlp[...]).astype(BF16)


def mlp_kernel(
    normed, rate, here, there, up_own, up_other, down_own, down_other,
    act_own, act_other, back_own, back_other, grad_moved, grad_normed,
):
    seen = here[...].astype(F32) + there[...].astype(F32)
    moved = (rate[:, :1] * seen).astype(BF16)
    grad_moved[...] = moved
    total = None
    for w_up, w_down, act, back in (
        (up_own, down_own, act_own, back_own),
        (up_other, down_other, act_other, back_other),
    ):
        up = mm(normed[...], w_up[...])
        square = up * up
        root = 0.7978845608028654
        t = jnp.tanh(root * (up + 0.044715 * (square * up)))
        act[...] = (0.5 * up * (1.0 + t)).astype(BF16)
        slope = 0.5 * (1.0 + t) + (0.5 * root) * up * (1.0 - t * t) * (1.0 + 0.134145 * square)
        grad_up = (mm_nt(moved, w_down[...]) * slope).astype(BF16)
        back[...] = grad_up
        part = mm_nt(grad_up, w_up[...])
        total = part if total is None else total + part
    grad_normed[...] = total.astype(BF16)


def mlp_grads_kernel(
    normed, grad_moved, act_own, act_other, back_own, back_other, down_own, down_other,
    gd_own, gd_other, gu_own, gu_other, moved,
):
    gd_other[...] = mm_tn(act_other[...], grad_moved[...]).astype(BF16)
    gd_own[...] = mm_tn(act_own[...], grad_moved[...])
    gu_other[...] = mm_tn(normed[...], back_other[...]).astype(BF16)
    gu_own[...] = mm_tn(normed[...], back_own[...])
    moved[...] = (mm(act_own[...], down_own[...]) + mm(act_other[...], down_other[...])).astype(BF16)


def norm_back(values, gain, grad):
    scale = lax.rsqrt(jnp.mean(values * values, axis=-1, keepdims=True) + EPS)
    scaled = grad * gain
    inner = jnp.mean(scaled * values, axis=-1, keepdims=True)
    back = scale * scaled - values * (scale * scale * scale * inner)
    return back, jnp.sum(grad * values * scale, axis=0, keepdims=True)


def attend_back_kernel(
    chosen_in, attended, gain_attn, gain_mlp, gn_here, gn_there, rate, seen_here, seen_there,
    query_in, key_in, value_in, probs_in, w_query, w_key, w_value, w_out,
    grad_attended_out, grad_query, grad_key, grad_value, grad_sum, small, mixed_back,
):
    slots, width = chosen_in.shape
    head = width // NH
    pair = 2 * head
    chosen = chosen_in[...].astype(F32)
    grad_normed_mlp = gn_here[...].astype(F32) + gn_there[...].astype(F32)
    grad_hidden, gain_grad = norm_back(chosen + attended[...], gain_mlp[...], grad_normed_mlp)
    small[1:2, :] = gain_grad
    seen = seen_here[...].astype(F32) + seen_there[...].astype(F32)
    grad_attended = (rate[:, :1] * seen + grad_hidden).astype(BF16)
    grad_attended_out[...] = grad_attended
    mixed_back[...] = mm_nt(grad_attended, w_out[...]).astype(BF16)
    first = lax.broadcasted_iota(jnp.int32, (slots, pair), 1) < head
    factor = head ** -0.5
    for p in range(NH // 2):
        cols = slice(p * pair, (p + 1) * pair)
        query = query_in[:, cols]
        keys = key_in[:, cols]
        values = value_in[:, cols]
        back = mixed_back[:, cols]
        parts = []
        for h in range(2):
            mine = first if h == 0 else ~first
            probs = probs_in[2 * p + h]
            grad_probs = mm_nt(jnp.where(mine, back, jnp.zeros_like(back)), values)
            gv = mm_tn(probs.astype(BF16), back)
            inner = jnp.sum(grad_probs * probs, axis=-1, keepdims=True)
            grad_logits = (probs * (grad_probs - inner)).astype(BF16)
            gq = mm(grad_logits, keys) * factor
            gk = mm_tn(grad_logits, query) * factor
            parts.append((gq, gk, gv))
        for out, a, b in zip((grad_query, grad_key, grad_value), parts[0], parts[1]):
            out[:, cols] = jnp.where(first, a, b).astype(BF16)
    grad_normed = (
        mm_nt(grad_query[...], w_query[...])
        + mm_nt(grad_key[...], w_key[...])
        + mm_nt(grad_value[...], w_value[...])
    )
    back, gain_grad = norm_back(chosen, gain_attn[...], grad_normed)
    small[0:1, :] = gain_grad
    grad_sum[...] = back + grad_hidden


def attend_grads_kernel(
    meta, normed, mixed, grad_query, grad_key, grad_value, grad_attended, own, other, full
):
    core = meta[1]
    width = normed.shape[1]
    half = width // 2
    quarter = half // 2
    cols = pl.ds(pl.multiple_of(meta[3] * half, 128), half)
    mine = pl.ds(pl.multiple_of(core * quarter, quarter), quarter)
    yours = pl.ds(pl.multiple_of((1 - core) * quarter, quarter), quarter)
    left = normed[:, cols]
    for m, grad in enumerate((grad_query, grad_key, grad_value, grad_attended)):
        if m == 3:
            left = mixed[:, cols]
        full[...] = mm_tn(left, grad[...])
        own[m * quarter : (m + 1) * quarter, :] = full[mine, :]
        other[m * quarter : (m + 1) * quarter, :] = full[yours, :].astype(BF16)


def slots_kernel(
    chosen_in, attended, rate_in, seen_here, seen_there, moved_here, moved_there, w_router, grad_sum,
    update, grad_chosen, grad_router,
):
    chosen = chosen_in[...].astype(F32)
    rate = rate_in[:, :1]
    seen = seen_here[...].astype(F32) + seen_there[...].astype(F32)
    delta = attended[...] + (moved_here[...].astype(F32) + moved_there[...].astype(F32))
    update[...] = (rate * delta).astype(BF16)
    score = rate * (1.0 - rate) * jnp.sum(seen * delta, axis=-1, keepdims=True)
    grad_chosen[...] = (grad_sum[...] + score * w_router[...].astype(F32)).astype(BF16)
    grad_router[...] = jnp.sum(score * chosen, axis=0, keepdims=True)


def swap(v, axis, size, bits):
    return lax.ppermute(v, axis, [(i, i ^ bits) for i in range(size)])


def pick(v, index):
    return lax.dynamic_index_in_dim(v, index, 0, keepdims=False)


def stages_of(size):
    stages, shift = [], 0
    while (1 << shift) < size:
        left = size >> shift
        radix = 4 if (shift > 0 and left >= 4) else 2
        stages.append((shift, radix))
        shift += radix.bit_length() - 1
    return stages


def scatter_sum(own, got, batch):
    index = lax.axis_index("batch")
    stages = stages_of(batch)
    shape = tuple(radix for _, radix in stages) + (own.shape[0] // batch, own.shape[1])
    current = (own.reshape(shape), got.reshape(shape))
    for shift, radix in stages:
        digit = (index >> shift) & (radix - 1)
        arrived = []
        for k in range(1, radix):
            piece = sum(pick(v, digit ^ k).astype(F32) for v in current).astype(BF16)
            arrived.append(swap(piece, "batch", batch, k << shift))
        current = (sum([pick(v, digit).astype(F32) for v in current] + [v.astype(F32) for v in arrived]),)
    return current[0].astype(BF16)


def gather_all(piece, batch):
    current = piece
    for shift, radix in reversed(stages_of(batch)):
        current = jnp.stack(
            [current] + [swap(current, "batch", batch, k << shift) for k in range(1, radix)]
        )
    return current


def digits_of(index, batch):
    return [(index >> shift) & (radix - 1) for shift, radix in stages_of(batch)]


def unscramble_kernel(index, *refs):
    half = len(refs) // 2
    for v, out in zip(refs[:half], refs[half:]):
        out[...] = v[...].reshape(out.shape).astype(F32)


def order_rows(gathered, batch):
    index = lax.axis_index("batch")
    stages = stages_of(batch)
    rows, width = gathered.shape[-2:]
    if batch != 8:
        for axis, digit in enumerate(digits_of(index, batch)):
            radix = gathered.shape[axis]
            gathered = jnp.take(gathered, jnp.arange(radix) ^ digit, axis=axis)
        return gathered.reshape(-1, width).astype(F32)
    meta = jnp.stack(digits_of(index, batch)).astype(jnp.int32)
    return pl.pallas_call(
        unscramble_kernel,
        grid_spec=pltpu.PrefetchScalarGridSpec(
            num_scalar_prefetch=1,
            grid=(2, 4),
            in_specs=[
                pl.BlockSpec((1, 1, rows, width), lambda i, j, m: (i ^ m[0], j ^ m[1], 0, 0))
            ],
            out_specs=[pl.BlockSpec((rows, width), lambda i, j, m: (i * 4 + j, 0))],
        ),
        out_shape=[jax.ShapeDtypeStruct((8 * rows, width), F32)],
    )(meta, gathered)[0]


def order_attention(gathered, batch, place):
    index = lax.axis_index("batch")
    rows, width = gathered.shape[-2:]
    core, side = place % 2, place // 2
    if batch != 8:
        for axis, digit in enumerate([core, side] + digits_of(index, batch)):
            radix = gathered.shape[axis]
            gathered = jnp.take(gathered, jnp.arange(radix) ^ digit, axis=axis)
        whole = gathered.astype(F32).reshape(2, 2, 4, -1, width).transpose(2, 1, 0, 3, 4)
        return [whole[m].reshape(-1, width) for m in range(4)]
    meta = jnp.stack([core, side] + digits_of(index, batch)).astype(jnp.int32)

    def source(m):
        def at(j, d):
            p = 2 * m + j % 2
            return (((j // 2) % 2) ^ d[0], (j // 4) ^ d[1], (p // 4) ^ d[2], (p % 4) ^ d[3], 0, 0)

        return pl.BlockSpec((1, 1, 1, 1, rows, width), at)

    return pl.pallas_call(
        unscramble_kernel,
        grid_spec=pltpu.PrefetchScalarGridSpec(
            num_scalar_prefetch=1,
            grid=(8,),
            in_specs=[source(m) for m in range(4)],
            out_specs=[pl.BlockSpec((rows, width), lambda j, d: (j, 0))] * 4,
        ),
        out_shape=[jax.ShapeDtypeStruct((8 * rows, width), F32)] * 4,
    )(meta, gathered, gathered, gathered, gathered)


def body(
    batch, tokens, lengths, picks, w_router, gain_attn, gain_mlp, w_query, w_key, w_value, w_out,
    w_up, w_down, cotangent,
):
    place = lax.axis_index("seq")
    core, side = place % 2, place // 2
    seqs, length, width = tokens.shape
    local = picks.shape[1]
    slots = 4 * local
    across = functools.partial(swap, axis="seq", size=4)
    row = lambda v: v.reshape(1, width)
    gain_attn, gain_mlp, w_router = row(gain_attn), row(gain_mlp), row(w_router)

    got = [picks] + [across(picks, bits=k) for k in (1, 2, 3)]
    up_other, down_other = across(w_up, bits=1), across(w_down, bits=1)
    count = pick(lengths, core) // 8
    meta = jnp.stack([place, core, count, side] + [place ^ k for k in range(4)]).astype(jnp.int32)
    stacked = jnp.stack(got)
    all_picks = jnp.concatenate([pick(stacked, place ^ a) for a in range(4)], axis=1)

    slot_shape = ((slots, width), BF16)
    wide = ((slots, width), F32)

    def select(rows):
        return call(
            select_kernel, [meta, *got, rows], [slot_shape, slot_shape],
            specs=[SMEM] + [VMEM] * 5, scratch=[pltpu.VMEM((slots, length), BF16)],
            flops=4 * slots * length * width,
        )

    own, other = select(tokens)
    here = own + across(other, bits=1)
    there = across(here, bits=2)
    own, other = select(cotangent)
    seen_here = own + across(other, bits=1)
    seen_there = across(seen_here, bits=2)

    (chosen, normed, query, keys, values, probs, mixed, attended, normed_mlp, rate) = call(
        attend_kernel,
        [meta, here, there, w_router, gain_attn, gain_mlp, w_query, w_key, w_value, w_out],
        [slot_shape] * 5 + [((NH, slots, slots), F32), slot_shape, wide, slot_shape, ((slots, 128), F32)],
        specs=[SMEM] + [VMEM] * 9,
        flops=8 * slots * width * width,
    )
    hidden_units = w_up.shape[1]
    act = ((slots, hidden_units), BF16)
    act_own, act_other, back_own, back_other, grad_moved, gn_here = call(
        mlp_kernel,
        [normed_mlp, rate, seen_here, seen_there, w_up, up_other, w_down, down_other],
        [act] * 4 + [slot_shape] * 2,
        flops=12 * slots * width * hidden_units,
    )
    gn_there = across(gn_here, bits=2)
    gd_own, gd_other, gu_own, gu_other, moved_here = call(
        mlp_grads_kernel,
        [normed_mlp, grad_moved, act_own, act_other, back_own, back_other, w_down, down_other],
        [
            ((hidden_units, width), F32), ((hidden_units, width), BF16),
            ((width, hidden_units), F32), ((width, hidden_units), BF16), slot_shape,
        ],
        flops=12 * slots * width * hidden_units,
    )
    moved_there = across(moved_here, bits=2)
    down_part = scatter_sum(gd_own, across(gd_other, bits=1), batch)
    up_part = scatter_sum(gu_own, across(gu_other, bits=1), batch)

    grad_attended, gq, gk, gv, grad_sum, small = call(
        attend_back_kernel,
        [
            chosen, attended, gain_attn, gain_mlp, gn_here, gn_there, rate, seen_here, seen_there,
            query, keys, values, probs, w_query, w_key, w_value, w_out,
        ],
        [slot_shape] * 4 + [wide, ((2, width), F32)],
        scratch=[pltpu.VMEM((slots, width), BF16)],
        flops=8 * slots * width * width,
    )
    ga_own, ga_other = call(
        attend_grads_kernel,
        [meta, normed, mixed, gq, gk, gv, grad_attended],
        [((width, width), F32), ((width, width), BF16)],
        specs=[SMEM] + [VMEM] * 6,
        scratch=[pltpu.VMEM((width // 2, width), F32)],
        flops=4 * slots * width * width,
    )
    attention_part = scatter_sum(ga_own, across(ga_other, bits=1), batch)
    update, grad_chosen, grad_router = call(
        slots_kernel,
        [chosen, attended, rate, seen_here, seen_there, moved_here, moved_there, w_router, grad_sum],
        [slot_shape, slot_shape, ((1, width), F32)],
    )

    def placed(rows, mine):
        return call(
            place_kernel, [meta, all_picks, rows, mine, across(mine, bits=1)],
            [(rows.shape, BF16)], specs=[SMEM] + [VMEM] * 4,
            flops=4 * slots * length * width,
        )[0]

    output = placed(tokens, update)
    grad_tokens = placed(cotangent, grad_chosen)

    vectors = jnp.concatenate([grad_router, small], axis=0)
    vectors = vectors + across(vectors, bits=1)
    for bit in range(batch.bit_length() - 1):
        vectors = vectors + swap(vectors, "batch", batch, 1 << bit)

    down_all = gather_all(down_part, batch)
    up_all = gather_all(up_part, batch)
    attention_all = gather_all(attention_part, batch)
    attention_all = jnp.stack([attention_all, across(attention_all, bits=2)])
    attention_all = jnp.stack([attention_all, across(attention_all, bits=1)])
    grad_query, grad_key, grad_value, grad_out = order_attention(attention_all, batch, place)
    return (
        output, grad_tokens, vectors[0], vectors[1], vectors[2],
        grad_query, grad_key, grad_value, grad_out,
        order_rows(up_all, batch), order_rows(down_all, batch),
    )


def solution(mesh):
    rows, whole = P("batch", "seq", None), P()
    return jax.shard_map(
        functools.partial(body, mesh.shape["batch"]),
        mesh=mesh,
        in_specs=(
            rows, P("batch"), P("batch", "seq"), whole, whole, whole, whole, whole, whole, whole,
            P(None, "seq"), P("seq", None), rows,
        ),
        out_specs=(
            rows, rows, whole, whole, whole, whole, whole, whole, whole,
            P(None, "seq"), P("seq", None),
        ),
        check_vma=False,
    )
```

```python
import functools

import jax
import jax.numpy as jnp
from jax import lax
from jax.experimental import pallas as pl
from jax.experimental.pallas import tpu as pltpu
from jax.sharding import PartitionSpec as P

NH = 12
Y, Z0, Z1 = 8, 9, 10
EPS = 1e-06
F32 = jnp.float32
BF16 = jnp.bfloat16
VMEM = pl.BlockSpec(memory_space=pltpu.VMEM)
SMEM = pl.BlockSpec(memory_space=pltpu.SMEM)
ANY = pl.BlockSpec(memory_space=pl.ANY)


def mm(a, b):
    return jnp.dot(a, b, preferred_element_type=F32)


def mm_nt(a, b):
    return lax.dot_general(a, b, (((1,), (1,)), ((), ())), preferred_element_type=F32)


def mm_tn(a, b):
    return lax.dot_general(a, b, (((0,), (0,)), ((), ())), preferred_element_type=F32)


def call(kernel, ins, outs, specs=None, scratch=(), vmem=12, flops=0, after=()):
    shapes = tuple(jax.ShapeDtypeStruct(shape, dtype) for shape, dtype in outs)
    moved = sum(v.size * v.dtype.itemsize for v in list(ins) + list(shapes))
    count, extra = len(ins), len(after)

    def run(*refs):
        kernel(*refs[:count], *refs[count + extra :])

    return pl.pallas_call(
        run,
        out_shape=shapes,
        in_specs=(specs or [VMEM] * count) + [ANY] * extra,
        out_specs=tuple(VMEM for _ in shapes),
        scratch_shapes=list(scratch),
        cost_estimate=pl.CostEstimate(flops=flops, bytes_accessed=moved, transcendentals=0),
        compiler_params=pltpu.CompilerParams(vmem_limit_bytes=vmem * 1024 * 1024),
    )(*ins, *after)


def select_kernel(meta, p0, p1, p2, p3, rows, own, other, hot_own, hot_other):
    core = meta[1]
    length = rows.shape[1]
    local = p0.shape[1]
    base = meta[0] * length
    down = lax.broadcasted_iota(jnp.int32, (local, local), 0)
    along = lax.broadcasted_iota(jnp.int32, (local, local), 1)
    places = lax.broadcasted_iota(jnp.int32, (local, length), 1)
    for seq, hot, out in ((1 - core, hot_other, other), (core, hot_own, own)):
        for k, part in enumerate((p0, p1, p2, p3)):
            row = part[pl.ds(seq, 1), :]
            column = jnp.sum(jnp.where(down == along, row, 0), axis=1, keepdims=True)
            at = pl.multiple_of(meta[4 + k] * local, local)
            hot[pl.ds(at, local), :] = jnp.where(column - base == places, 1.0, 0.0).astype(BF16)
        out[...] = mm(hot[...], rows[seq]).astype(BF16)


def select_again_kernel(meta, hot_own, hot_other, rows, own, other):
    core = meta[1]
    other[...] = mm(hot_other[...], rows[1 - core]).astype(BF16)
    own[...] = mm(hot_own[...], rows[core]).astype(BF16)


def place_kernel(meta, hot_own, hot_other, rows, own, other, out):
    core = meta[1]
    for seq, hot, update in ((core, hot_own, own), (1 - core, hot_other, other)):
        out[seq] = (rows[seq].astype(F32) + mm_tn(hot[...], update[...])).astype(BF16)


def attend_kernel(
    meta, here, there, w_router, gain_attn, gain_mlp, w_query, w_key, w_value, w_out,
    chosen_out, normed_out, query_out, key_out, value_out, probs_out, mixed_out, attended_out,
    normed_mlp_out, rate_out,
):
    count = meta[2]
    slots, width = here.shape
    chosen = here[...].astype(F32) + there[...].astype(F32)
    chosen_out[...] = chosen.astype(BF16)
    score = jnp.sum(chosen * w_router[...].astype(F32), axis=-1, keepdims=True)
    rate = jax.nn.sigmoid(score)
    valid = lax.broadcasted_iota(jnp.int32, (slots, 1), 0) < count
    rate_out[...] = jnp.broadcast_to(jnp.where(valid, rate, 0.0), rate_out.shape)
    scale = lax.rsqrt(jnp.mean(chosen * chosen, axis=-1, keepdims=True) + EPS)
    normed = (chosen * scale * gain_attn[...]).astype(BF16)
    normed_out[...] = normed
    query_out[...] = mm(normed, w_query[...]).astype(BF16)
    key_out[...] = mm(normed, w_key[...]).astype(BF16)
    value_out[...] = mm(normed, w_value[...]).astype(BF16)
    head = width // NH
    pair = 2 * head
    i = lax.broadcasted_iota(jnp.int32, (slots, slots), 0)
    j = lax.broadcasted_iota(jnp.int32, (slots, slots), 1)
    allowed = (j <= i) & (j < count)
    first = lax.broadcasted_iota(jnp.int32, (slots, pair), 1) < head
    for p in range(NH // 2):
        cols = slice(p * pair, (p + 1) * pair)
        query = query_out[:, cols]
        keys = key_out[:, cols]
        values = value_out[:, cols]
        halves = []
        for h in range(2):
            mine = first if h == 0 else ~first
            logits = mm_nt(jnp.where(mine, query, jnp.zeros_like(query)), keys) * (head ** -0.5)
            logits = jnp.where(allowed, logits, -1e30)
            expd = jnp.exp(logits - jnp.max(logits, axis=-1, keepdims=True))
            probs = expd / jnp.sum(expd, axis=-1, keepdims=True)
            probs_out[2 * p + h] = probs
            halves.append(mm(probs.astype(BF16), values))
        mixed_out[:, cols] = jnp.where(first, halves[0], halves[1]).astype(BF16)
    attended = mm(mixed_out[...], w_out[...])
    attended_out[...] = attended
    hidden = chosen + attended
    scale = lax.rsqrt(jnp.mean(hidden * hidden, axis=-1, keepdims=True) + EPS)
    normed_mlp_out[...] = (hidden * scale * gain_mlp[...]).astype(BF16)


def mlp_kernel(
    normed, rate, here, there, up_own, up_other, down_own, down_other,
    act_own, act_other, back_own, back_other, grad_moved, grad_normed,
):
    seen = here[...].astype(F32) + there[...].astype(F32)
    moved = (rate[:, :1] * seen).astype(BF16)
    grad_moved[...] = moved
    total = None
    for w_up, w_down, act, back in (
        (up_own, down_own, act_own, back_own),
        (up_other, down_other, act_other, back_other),
    ):
        up = mm(normed[...], w_up[...])
        square = up * up
        root = 0.7978845608028654
        t = jnp.tanh(root * (up + 0.044715 * (square * up)))
        act[...] = (0.5 * up * (1.0 + t)).astype(BF16)
        slope = 0.5 * (1.0 + t) + (0.5 * root) * up * (1.0 - t * t) * (1.0 + 0.134145 * square)
        grad_up = (mm_nt(moved, w_down[...]) * slope).astype(BF16)
        back[...] = grad_up
        part = mm_nt(grad_up, w_up[...])
        total = part if total is None else total + part
    grad_normed[...] = total.astype(BF16)


def mlp_grads_kernel(
    normed, grad_moved, act_own, act_other, back_own, back_other, down_own, down_other,
    gd_own, gd_other, gu_own, gu_other, moved,
):
    gd_other[...] = mm_tn(act_other[...], grad_moved[...]).astype(BF16)
    gd_own[...] = mm_tn(act_own[...], grad_moved[...])
    gu_other[...] = mm_tn(normed[...], back_other[...]).astype(BF16)
    gu_own[...] = mm_tn(normed[...], back_own[...])
    moved[...] = (mm(act_own[...], down_own[...]) + mm(act_other[...], down_other[...])).astype(BF16)


def norm_back(values, gain, grad):
    scale = lax.rsqrt(jnp.mean(values * values, axis=-1, keepdims=True) + EPS)
    scaled = grad * gain
    inner = jnp.mean(scaled * values, axis=-1, keepdims=True)
    back = scale * scaled - values * (scale * scale * scale * inner)
    return back, jnp.sum(grad * values * scale, axis=0, keepdims=True)


def attend_back_kernel(
    chosen_in, attended, gain_attn, gain_mlp, gn_here, gn_there, rate, seen_here, seen_there,
    query_in, key_in, value_in, probs_in, w_query, w_key, w_value, w_out,
    grad_attended_out, grad_query, grad_key, grad_value, grad_sum, small, mixed_back,
):
    small[...] = jnp.zeros_like(small)
    slots, width = chosen_in.shape
    head = width // NH
    pair = 2 * head
    chosen = chosen_in[...].astype(F32)
    grad_normed_mlp = gn_here[...].astype(F32) + gn_there[...].astype(F32)
    grad_hidden, gain_grad = norm_back(chosen + attended[...], gain_mlp[...], grad_normed_mlp)
    small[2:3, :] = gain_grad
    seen = seen_here[...].astype(F32) + seen_there[...].astype(F32)
    grad_attended = (rate[:, :1] * seen + grad_hidden).astype(BF16)
    grad_attended_out[...] = grad_attended
    mixed_back[...] = mm_nt(grad_attended, w_out[...]).astype(BF16)
    first = lax.broadcasted_iota(jnp.int32, (slots, pair), 1) < head
    factor = head ** -0.5
    for p in range(NH // 2):
        cols = slice(p * pair, (p + 1) * pair)
        query = query_in[:, cols]
        keys = key_in[:, cols]
        values = value_in[:, cols]
        back = mixed_back[:, cols]
        parts = []
        for h in range(2):
            mine = first if h == 0 else ~first
            probs = probs_in[2 * p + h]
            grad_probs = mm_nt(jnp.where(mine, back, jnp.zeros_like(back)), values)
            gv = mm_tn(probs.astype(BF16), back)
            inner = jnp.sum(grad_probs * probs, axis=-1, keepdims=True)
            grad_logits = (probs * (grad_probs - inner)).astype(BF16)
            gq = mm(grad_logits, keys) * factor
            gk = mm_tn(grad_logits, query) * factor
            parts.append((gq, gk, gv))
        for out, a, b in zip((grad_query, grad_key, grad_value), parts[0], parts[1]):
            out[:, cols] = jnp.where(first, a, b).astype(BF16)
    grad_normed = (
        mm_nt(grad_query[...], w_query[...])
        + mm_nt(grad_key[...], w_key[...])
        + mm_nt(grad_value[...], w_value[...])
    )
    back, gain_grad = norm_back(chosen, gain_attn[...], grad_normed)
    small[1:2, :] = gain_grad
    grad_sum[...] = back + grad_hidden


def attend_grads_kernel(
    meta, normed, mixed, grad_query, grad_key, grad_value, grad_attended, own, other, full
):
    core = meta[1]
    width = normed.shape[1]
    half = width // 2
    quarter = half // 2
    cols = pl.ds(pl.multiple_of(meta[3] * half, 128), half)
    mine = pl.ds(pl.multiple_of(core * quarter, quarter), quarter)
    yours = pl.ds(pl.multiple_of((1 - core) * quarter, quarter), quarter)
    left = normed[:, cols]
    for m, grad in enumerate((grad_query, grad_key, grad_value, grad_attended)):
        if m == 3:
            left = mixed[:, cols]
        full[...] = mm_tn(left, grad[...])
        own[m * quarter : (m + 1) * quarter, :] = full[mine, :]
        other[m * quarter : (m + 1) * quarter, :] = full[yours, :].astype(BF16)


def slots_kernel(
    chosen_in, attended, rate_in, seen_here, seen_there, moved_here, moved_there, w_router, grad_sum,
    small, update, grad_chosen, vectors,
):
    chosen = chosen_in[...].astype(F32)
    rate = rate_in[:, :1]
    seen = seen_here[...].astype(F32) + seen_there[...].astype(F32)
    delta = attended[...] + (moved_here[...].astype(F32) + moved_there[...].astype(F32))
    update[...] = (rate * delta).astype(BF16)
    score = rate * (1.0 - rate) * jnp.sum(seen * delta, axis=-1, keepdims=True)
    grad_chosen[...] = (grad_sum[...] + score * w_router[...].astype(F32)).astype(BF16)
    vectors[...] = jnp.zeros_like(vectors)
    vectors[0:1, :] = jnp.sum(score * chosen, axis=0, keepdims=True)
    vectors[1:3, :] = small[1:3, :]


def reduce_kernel(plan, gots, sends, meta, *refs):
    keeps, refs = refs[: len(plan)], refs[len(plan) :]
    got, refs = refs[:gots], refs[gots:]
    send, kept = refs[:sends], refs[sends:]
    for keep, new, (rows, bit, g, g_row, t, t_row) in zip(keeps, kept, plan):
        half = rows // 2
        mine = pl.multiple_of(meta[bit] * half, half)
        yours = pl.multiple_of((1 - meta[bit]) * half, half)
        send[t][t_row : t_row + half, :] = (
            keep[pl.ds(yours, half), :] + got[g][pl.ds(g_row + yours, half), :].astype(F32)
        ).astype(BF16)
        new[...] = keep[pl.ds(mine, half), :] + got[g][pl.ds(g_row + mine, half), :].astype(F32)


def split_vectors(v):
    high = v.astype(BF16).astype(F32)
    return jnp.concatenate([high, (v - high).astype(BF16).astype(F32)], axis=0)


def join_vectors(v):
    return v[:8, :] + v[8:, :]


def reduce_small_kernel(plan, gots, sends, meta, *refs):
    vectors, refs = refs[0], refs[1:]
    out = refs[-1]
    reduce_kernel(plan, gots, sends, meta, *refs[:-1])
    got = refs[len(plan)]
    own = join_vectors(split_vectors(vectors[...])) + join_vectors(got[got.shape[0] - 16 :, :].astype(F32))
    out[...] = own
    send = refs[len(plan) + gots]
    send[send.shape[0] - 16 :, :] = split_vectors(own).astype(BF16)


def attention_first_kernel(plan, meta, vectors, own, got, send_a, send_b, keep_a, keep_b, out):
    for n, (send, keep) in enumerate(((send_a, keep_a), (send_b, keep_b))):
        rows, bit, _, row, _, _ = plan[n]
        half = rows // 2
        mine = pl.ds(pl.multiple_of(row + meta[bit] * half, half), half)
        yours = pl.ds(pl.multiple_of(row + (1 - meta[bit]) * half, half), half)
        send[:half, :] = (own[yours, :] + got[yours, :].astype(F32)).astype(BF16)
        keep[...] = own[mine, :] + got[mine, :].astype(F32)
    out[...] = vectors[...]
    send_a[send_a.shape[0] - 16 :, :] = split_vectors(vectors[...]).astype(BF16)


def finish_kernel(vectors, first, second, got, cur, out):
    rows = first.shape[0]
    cur[:rows, :] = (first[...] + got[:rows, :].astype(F32)).astype(BF16)
    cur[rows:, :] = (second[...] + got[rows : 2 * rows, :].astype(F32)).astype(BF16)
    if vectors is not None:
        own = join_vectors(split_vectors(vectors[...]))
        out[...] = own + join_vectors(got[2 * rows :, :].astype(F32))


def join_kernel(plan, meta, *refs):
    count = len(plan)
    for (rows, bit, row, got_row), own, got, out in zip(
        plan, refs[:count], refs[count : 2 * count], refs[2 * count :]
    ):
        mine = pl.multiple_of(meta[bit] * rows, rows)
        yours = pl.multiple_of((1 - meta[bit]) * rows, rows)
        out[pl.ds(mine, rows), :] = own[row : row + rows, :].astype(out.dtype)
        out[pl.ds(yours, rows), :] = got[got_row : got_row + rows, :].astype(out.dtype)


def join_both_kernel(meta, own_a, own_b, got_a, got_b, out_a, out_b, both):
    rows = own_a.shape[0]
    for at, bit, own, got, out in ((0, Z0, own_a, got_a, out_a), (2 * rows, Y, own_b, got_b, out_b)):
        mine = pl.multiple_of(meta[bit] * rows, rows)
        yours = pl.multiple_of((1 - meta[bit]) * rows, rows)
        out[pl.ds(mine, rows), :] = own[...]
        out[pl.ds(yours, rows), :] = got[...]
        both[at : at + 2 * rows, :] = out[...]


def stack_kernel(got_a, got_b, late):
    rows = got_a.shape[0]
    late[:rows, :] = got_a[...]
    late[rows:, :] = got_b[...]


def attention_kernel(meta, *refs):
    pieces, outs = refs[:8], refs[8:]
    core, side, y, z0 = meta[1], meta[3], meta[Y], meta[Z0]
    part = outs[0].shape[0] // 4
    for n in range(8):
        other_core, other_side, late = n // 4, (n // 2) % 2, n % 2
        quarter = 2 * (side ^ other_side) + (core ^ other_core)
        for packet, bit in ((0, y), (1, z0)):
            index = bit ^ late
            block = pieces[n][packet * part : (packet + 1) * part, :].astype(F32)
            at = pl.multiple_of(quarter * part, 8)
            for which in range(2):
                @pl.when(index == which)
                def _(block=block, at=at, out=outs[2 * packet + which]):
                    out[pl.ds(at, part), :] = block


def swap(v, axis, size, bits):
    return lax.ppermute(v, axis, [(i, i ^ bits) for i in range(size)])


def pick(v, index):
    return lax.dynamic_index_in_dim(v, index, 0, keepdims=False)


def stages_of(size):
    stages, shift = [], 0
    while (1 << shift) < size:
        left = size >> shift
        radix = 4 if (shift > 0 and left >= 4) else 2
        stages.append((shift, radix))
        shift += radix.bit_length() - 1
    return stages


def scatter_sum(own, got, batch):
    index = lax.axis_index("batch")
    stages = stages_of(batch)
    shape = tuple(radix for _, radix in stages) + (own.shape[0] // batch, own.shape[1])
    current = (own.reshape(shape), got.reshape(shape))
    for shift, radix in stages:
        digit = (index >> shift) & (radix - 1)
        arrived = []
        for k in range(1, radix):
            piece = sum(pick(v, digit ^ k).astype(F32) for v in current).astype(BF16)
            arrived.append(swap(piece, "batch", batch, k << shift))
        current = (sum([pick(v, digit).astype(F32) for v in current] + [v.astype(F32) for v in arrived]),)
    return current[0].astype(BF16)


def gather_all(piece, batch):
    current = piece
    for shift, radix in reversed(stages_of(batch)):
        current = jnp.stack(
            [current] + [swap(current, "batch", batch, k << shift) for k in range(1, radix)]
        )
    return current


def digits_of(index, batch):
    return [(index >> shift) & (radix - 1) for shift, radix in stages_of(batch)]


def unscramble_kernel(index, *refs):
    half = len(refs) // 2
    for v, out in zip(refs[:half], refs[half:]):
        out[...] = v[...].reshape(out.shape).astype(F32)


def order_rows(gathered, batch):
    index = lax.axis_index("batch")
    stages = stages_of(batch)
    rows, width = gathered.shape[-2:]
    if batch != 8:
        for axis, digit in enumerate(digits_of(index, batch)):
            radix = gathered.shape[axis]
            gathered = jnp.take(gathered, jnp.arange(radix) ^ digit, axis=axis)
        return gathered.reshape(-1, width).astype(F32)
    meta = jnp.stack(digits_of(index, batch)).astype(jnp.int32)
    return pl.pallas_call(
        unscramble_kernel,
        grid_spec=pltpu.PrefetchScalarGridSpec(
            num_scalar_prefetch=1,
            grid=(2, 4),
            in_specs=[
                pl.BlockSpec((1, 1, rows, width), lambda i, j, m: (i ^ m[0], j ^ m[1], 0, 0))
            ],
            out_specs=[pl.BlockSpec((rows, width), lambda i, j, m: (i * 4 + j, 0))],
        ),
        out_shape=[jax.ShapeDtypeStruct((8 * rows, width), F32)],
    )(meta, gathered)[0]


def order_attention(gathered, batch, place):
    index = lax.axis_index("batch")
    rows, width = gathered.shape[-2:]
    core, side = place % 2, place // 2
    if batch != 8:
        for axis, digit in enumerate([core, side] + digits_of(index, batch)):
            radix = gathered.shape[axis]
            gathered = jnp.take(gathered, jnp.arange(radix) ^ digit, axis=axis)
        whole = gathered.astype(F32).reshape(2, 2, 4, -1, width).transpose(2, 1, 0, 3, 4)
        return [whole[m].reshape(-1, width) for m in range(4)]
    meta = jnp.stack([core, side] + digits_of(index, batch)).astype(jnp.int32)

    def source(m):
        def at(j, d):
            p = 2 * m + j % 2
            return (((j // 2) % 2) ^ d[0], (j // 4) ^ d[1], (p // 4) ^ d[2], (p % 4) ^ d[3], 0, 0)

        return pl.BlockSpec((1, 1, 1, 1, rows, width), at)

    return pl.pallas_call(
        unscramble_kernel,
        grid_spec=pltpu.PrefetchScalarGridSpec(
            num_scalar_prefetch=1,
            grid=(8,),
            in_specs=[source(m) for m in range(4)],
            out_specs=[pl.BlockSpec((rows, width), lambda j, d: (j, 0))] * 4,
        ),
        out_shape=[jax.ShapeDtypeStruct((8 * rows, width), F32)] * 4,
    )(meta, gathered, gathered, gathered, gathered)


def body(
    batch, tokens, lengths, picks, w_router, gain_attn, gain_mlp, w_query, w_key, w_value, w_out,
    w_up, w_down, cotangent,
):
    place = lax.axis_index("seq")
    core, side = place % 2, place // 2
    seqs, length, width = tokens.shape
    local = picks.shape[1]
    slots = 4 * local
    across = functools.partial(swap, axis="seq", size=4)
    row = lambda v: v.reshape(1, width)
    gain_attn, gain_mlp, w_router = row(gain_attn), row(gain_mlp), row(w_router)

    index = lax.axis_index("batch")
    along = lambda v, bit: swap(v, "batch", batch, 1 << bit)
    got = [picks] + [across(picks, bits=k) for k in (1, 2, 3)]
    up_other, down_other = across(w_up, bits=1), across(w_down, bits=1)
    count = pick(lengths, core) // 8
    meta = jnp.stack(
        [place, core, count, side] + [place ^ k for k in range(4)] + [(index >> k) & 1 for k in range(3)]
    ).astype(jnp.int32)

    slot_shape = ((slots, width), BF16)
    wide = ((slots, width), F32)
    hot_shape = ((slots, length), BF16)

    own, other, hot_own, hot_other = call(
        select_kernel, [meta, *got, tokens], [slot_shape] * 2 + [hot_shape] * 2,
        specs=[SMEM] + [VMEM] * 5, flops=4 * slots * length * width,
    )
    here = own + across(other, bits=1)
    there = across(here, bits=2)
    own, other = call(
        select_again_kernel, [meta, hot_own, hot_other, cotangent], [slot_shape] * 2,
        specs=[SMEM] + [VMEM] * 3, flops=4 * slots * length * width, after=[here],
    )
    seen_here = own + across(other, bits=1)
    seen_there = across(seen_here, bits=2)

    (chosen, normed, query, keys, values, probs, mixed, attended, normed_mlp, rate) = call(
        attend_kernel,
        [meta, here, there, w_router, gain_attn, gain_mlp, w_query, w_key, w_value, w_out],
        [slot_shape] * 5 + [((NH, slots, slots), F32), slot_shape, wide, slot_shape, ((slots, 128), F32)],
        specs=[SMEM] + [VMEM] * 9, flops=8 * slots * width * width, after=[seen_here],
    )
    hidden_units = w_up.shape[1]
    act = ((slots, hidden_units), BF16)
    act_own, act_other, back_own, back_other, grad_moved, gn_here = call(
        mlp_kernel,
        [normed_mlp, rate, seen_here, seen_there, w_up, up_other, w_down, down_other],
        [act] * 4 + [slot_shape] * 2,
        flops=12 * slots * width * hidden_units,
    )
    gn_there = across(gn_here, bits=2)
    gd_own, gd_other, gu_own, gu_other, moved_here = call(
        mlp_grads_kernel,
        [normed_mlp, grad_moved, act_own, act_other, back_own, back_other, w_down, down_other],
        [
            ((hidden_units, width), F32), ((hidden_units, width), BF16),
            ((width, hidden_units), F32), ((width, hidden_units), BF16), slot_shape,
        ],
        flops=12 * slots * width * hidden_units,
    )
    gd_got, gu_got = across(gd_other, bits=1), across(gu_other, bits=1)
    moved_there = across(moved_here, bits=2)

    def attend_back(after):
        grad_attended, gq, gk, gv, grad_sum, small = call(
            attend_back_kernel,
            [
                chosen, attended, gain_attn, gain_mlp, gn_here, gn_there, rate, seen_here, seen_there,
                query, keys, values, probs, w_query, w_key, w_value, w_out,
            ],
            [slot_shape] * 4 + [wide, ((8, width), F32)],
            scratch=[pltpu.VMEM((slots, width), BF16)],
            flops=8 * slots * width * width, after=after,
        )
        ga_own, ga_other = call(
            attend_grads_kernel,
            [meta, normed, mixed, gq, gk, gv, grad_attended],
            [((width, width), F32), ((width, width), BF16)],
            specs=[SMEM] + [VMEM] * 6,
            scratch=[pltpu.VMEM((width // 2, width), F32)],
            flops=4 * slots * width * width,
        )
        ga_got = across(ga_other, bits=1)
        update, grad_chosen, vectors = call(
            slots_kernel,
            [chosen, attended, rate, seen_here, seen_there, moved_here, moved_there, w_router, grad_sum, small],
            [slot_shape, slot_shape, ((8, width), F32)], after=[ga_own],
        )
        vectors = vectors + across(vectors, bits=1)
        return ga_own, ga_got, update, grad_chosen, vectors

    def placed(rows, mine, after=()):
        return call(
            place_kernel, [meta, hot_own, hot_other, rows, mine, across(mine, bits=1)],
            [(rows.shape, BF16)], specs=[SMEM] + [VMEM] * 5,
            flops=4 * slots * length * width, after=after,
        )[0]

    if batch != 8:
        ga_own, ga_got, update, grad_chosen, vectors = attend_back([])
        for bit in range(batch.bit_length() - 1):
            vectors = vectors + along(vectors, bit)
        down_all = gather_all(scatter_sum(gd_own, gd_got, batch), batch)
        up_all = gather_all(scatter_sum(gu_own, gu_got, batch), batch)
        attention_all = gather_all(scatter_sum(ga_own, ga_got, batch), batch)
        attention_all = jnp.stack([attention_all, across(attention_all, bits=2)])
        attention_all = jnp.stack([attention_all, across(attention_all, bits=1)])
        return (
            placed(tokens, update), placed(cotangent, grad_chosen), vectors[0], vectors[1], vectors[2],
            *order_attention(attention_all, batch, place),
            order_rows(up_all, batch), order_rows(down_all, batch),
        )

    def reduce(keeps, gots, plan, sends, after=(), vectors=None):
        kernel = functools.partial(reduce_kernel, plan, len(gots), len(sends))
        outs = [((n, width), BF16) for n in sends] + [((p[0] // 2, width), F32) for p in plan]
        ins = [meta, *keeps, *gots]
        if vectors is not None:
            kernel = functools.partial(reduce_small_kernel, plan, len(gots), len(sends))
            ins = [meta, vectors, *keeps, *gots]
            outs.append(((8, width), F32))
        return call(kernel, ins, outs, specs=[SMEM] + [VMEM] * (len(ins) - 1), after=after)

    def join(plan, own, got, dtype, after=()):
        return call(
            functools.partial(join_kernel, plan), [meta, *own, *got],
            [((2 * p[0], width), dtype) for p in plan], specs=[SMEM] + [VMEM] * (2 * len(plan)), after=after,
        )

    n = width
    d_send, u_send, d_keep, u_keep = reduce(
        [gd_own, gu_own], [gd_got, gu_got], [(n, Y, 0, 0, 0, 0), (n, Z0, 1, 0, 1, 0)], [n // 2] * 2
    )
    d_got, u_got = along(d_send, 0), along(u_send, 1)
    ga_own, ga_got, update, grad_chosen, vectors = attend_back([d_keep])
    d_send, u_send, d_keep, u_keep = reduce(
        [d_keep, u_keep], [d_got, u_got], [(n // 2, Z0, 0, 0, 0, 0), (n // 2, Y, 1, 0, 1, 0)], [n // 4] * 2,
        after=[update],
    )
    d_got, u_got = along(d_send, 1), along(u_send, 0)
    half = n // 2
    a_first = [(half, Y, 0, 0, 0, 0), (half, Z0, 0, half, 1, 0)]
    a_send, b_send, a_keep, b_keep, vectors = call(
        functools.partial(attention_first_kernel, a_first),
        [meta, vectors, ga_own, ga_got],
        [((half // 2 + 16, width), BF16), ((half // 2, width), BF16)] + [((half // 2, width), F32)] * 2
        + [((8, width), F32)],
        specs=[SMEM] + [VMEM] * 3, after=[d_keep],
    )
    a_got, b_got = along(a_send, 0), along(b_send, 1)
    output = placed(tokens, update, after=[a_keep])
    send, d_keep, u_keep = reduce(
        [d_keep, u_keep], [d_got, u_got], [(n // 4, Z1, 0, 0, 0, 0), (n // 4, Z1, 1, 0, 0, n // 8)], [n // 4],
        after=[output],
    )
    du_got = along(send, 2)
    a_send, b_send, a_keep, b_keep, vectors = reduce(
        [a_keep, b_keep], [a_got, b_got], [(half // 2, Z0, 0, 0, 0, 0), (half // 2, Y, 1, 0, 1, 0)],
        [half // 4 + 16, half // 4], vectors=vectors, after=[d_keep],
    )
    a_got, b_got = along(a_send, 1), along(b_send, 0)
    grad_tokens = placed(cotangent, grad_chosen, after=[a_keep])
    cur = call(
        lambda *r: finish_kernel(None, *r, None), [d_keep, u_keep, du_got], [((n // 4, width), BF16)],
        after=[grad_tokens],
    )[0]
    du_got = along(cur, 2)
    send, a_keep, b_keep, vectors = reduce(
        [a_keep, b_keep], [a_got, b_got], [(half // 4, Z1, 0, 0, 0, 0), (half // 4, Z1, 1, 0, 0, half // 8)],
        [half // 4 + 16], vectors=vectors, after=[cur],
    )
    ab_got = along(send, 2)
    d_all, u_all = join(
        [(n // 8, Z1, 0, 0), (n // 8, Z1, n // 8, n // 8)], [cur, cur], [du_got, du_got], BF16, after=[a_keep]
    )
    d_got, u_got = along(d_all, 1), along(u_all, 0)
    ab, vectors = call(
        finish_kernel, [vectors, a_keep, b_keep, ab_got], [((half // 4, width), BF16), ((8, width), F32)],
        after=[d_all],
    )
    ab_got = along(ab, 2)
    d_all, u_all = join(
        [(n // 4, Z0, 0, 0), (n // 4, Y, 0, 0)], [d_all, u_all], [d_got, u_got], BF16, after=[ab]
    )
    d_got, u_got = along(d_all, 0), along(u_all, 1)
    a_all, b_all = join(
        [(half // 8, Z1, 0, 0), (half // 8, Z1, half // 8, half // 8)], [ab, ab], [ab_got, ab_got], BF16,
        after=[d_all],
    )
    a_got, b_got = along(a_all, 1), along(b_all, 0)
    a_all, b_all, early = call(
        join_both_kernel, [meta, a_all, b_all, a_got, b_got],
        [((half // 2, width), BF16)] * 2 + [((half, width), BF16)], specs=[SMEM] + [VMEM] * 4,
    )
    a_got, b_got = along(a_all, 0), along(b_all, 1)
    early_side = across(early, bits=2)
    early_core = across(early, bits=1)
    grad_down, grad_up = join(
        [(n // 2, Y, 0, 0), (n // 2, Z0, 0, 0)], [d_all, u_all], [d_got, u_got], F32, after=[early]
    )
    late = call(stack_kernel, [a_got, b_got], [((half, width), BF16)], after=[grad_down])[0]
    late_side = across(late, bits=2)
    late_core = across(late, bits=1)
    early_far = across(early_side, bits=1)
    late_far = across(late_side, bits=1)
    grads = call(
        attention_kernel,
        [meta, early, late, early_side, late_side, early_core, late_core, early_far, late_far],
        [((width, width), F32)] * 4, specs=[SMEM] + [VMEM] * 8,
    )
    return (output, grad_tokens, vectors[0], vectors[1], vectors[2], *grads, grad_up, grad_down)


def solution(mesh):
    rows, whole = P("batch", "seq", None), P()
    return jax.shard_map(
        functools.partial(body, mesh.shape["batch"]),
        mesh=mesh,
        in_specs=(
            rows, P("batch"), P("batch", "seq"), whole, whole, whole, whole, whole, whole, whole,
            P(None, "seq"), P("seq", None), rows,
        ),
        out_specs=(
            rows, rows, whole, whole, whole, whole, whole, whole, whole,
            P(None, "seq"), P("seq", None),
        ),
        check_vma=False,
    )
```

```python
import functools

import jax
import jax.numpy as jnp
from jax import lax
from jax.experimental import pallas as pl
from jax.experimental.pallas import tpu as pltpu
from jax.sharding import PartitionSpec as P

NH = 12
Y, Z0, Z1 = 8, 9, 10
ORDER = (
    "F AB SL R2 FA D3 A2 A3 P2 R2U U3 A4 D4 P1 A5 U4 A6 U5 D5 AT0 XC UU DU AT1"
).split()
WORK = {'P1': 2000, 'AB': 100, 'A5': 8000, 'D5': 4000, 'U5': 8000, 'U4': 2000, 'D3': 300, 'SL': 8000, 'UU': 300, 'DU': 1000, 'P2': 4000, 'R2': 4000, 'AT0': 2000, 'A6': 300, 'SA': 8000, 'A4': 4000, 'ML': 100, 'A2': 300, 'R2U': 600, 'A3': 1000}
HOLD = {'A2': ['u1'], 'P2': ['d3'], 'U5': ['x1'], 'U4': ['b6'], 'A3': ['up'], 'A6': ['ce'], 'UU': ['d6']}
EPS = 1e-06
F32 = jnp.float32
BF16 = jnp.bfloat16
VMEM = pl.BlockSpec(memory_space=pltpu.VMEM)
SMEM = pl.BlockSpec(memory_space=pltpu.SMEM)
ANY = pl.BlockSpec(memory_space=pl.ANY)
HBM = pl.BlockSpec(memory_space=pltpu.HBM)


def mm(a, b):
    return jnp.dot(a, b, preferred_element_type=F32)


def mm_nt(a, b):
    return lax.dot_general(a, b, (((1,), (1,)), ((), ())), preferred_element_type=F32)


def mm_tn(a, b):
    return lax.dot_general(a, b, (((0,), (0,)), ((), ())), preferred_element_type=F32)


def call(
    tag, kernel, ins, outs, specs=None, scratch=(), vmem=12, after=(), name=None, token=False,
    out_specs=None, aliases=None,
):
    shapes = [jax.ShapeDtypeStruct(shape, dtype) for shape, dtype in outs]
    results = len(shapes)
    out_specs = list(out_specs or [VMEM] * results)
    if token:
        shapes.append(jax.ShapeDtypeStruct((8, 128), F32))
        out_specs.append(VMEM)
    count, extra = len(ins), len(after)

    def run(*refs):
        rest = refs[count + extra :]
        if token:
            rest[results][...] = jnp.zeros((8, 128), F32)
            rest = rest[:results] + rest[results + 1 :]
        kernel(*refs[:count], *rest)

    return pl.pallas_call(
        run,
        out_shape=tuple(shapes),
        in_specs=(specs or [VMEM] * count) + [ANY] * extra,
        out_specs=tuple(out_specs),
        scratch_shapes=list(scratch),
        input_output_aliases=aliases or {},
        name=name or getattr(kernel, "func", kernel).__name__,
        cost_estimate=pl.CostEstimate(flops=1 + WORK.get(tag, 0) * 1_000_000, bytes_accessed=1, transcendentals=0),
        compiler_params=pltpu.CompilerParams(vmem_limit_bytes=vmem * 1024 * 1024),
    )(*ins, *after)


def select_kernel(meta, p1, p2, p3, picks, rows, own, other, hot_own, hot_other, local_rows, p0, sems):
    core = meta[1]
    copies = [
        pltpu.make_async_copy(picks, p0, sems.at[0]),
        pltpu.make_async_copy(rows.at[1 - core], local_rows.at[0], sems.at[1]),
        pltpu.make_async_copy(rows.at[core], local_rows.at[1], sems.at[2]),
    ]
    for copy in copies:
        copy.start()
    length = rows.shape[1]
    local = p1.shape[1]
    base = meta[0] * length
    down = lax.broadcasted_iota(jnp.int32, (local, local), 0)
    along = lax.broadcasted_iota(jnp.int32, (local, local), 1)
    places = lax.broadcasted_iota(jnp.int32, (local, length), 1)
    for k, part in ((1, p1), (2, p2), (3, p3), (0, p0)):
        if k == 0:
            copies[0].wait()
        at = pl.multiple_of(meta[4 + k] * local, local)
        for seq, hot in ((1 - core, hot_other), (core, hot_own)):
            row = part[pl.ds(seq, 1), :]
            column = jnp.sum(jnp.where(down == along, row, 0), axis=1, keepdims=True)
            hot[pl.ds(at, local), :] = jnp.where(column - base == places, 1.0, 0.0).astype(BF16)
    copies[1].wait()
    other[...] = mm(hot_other[...], local_rows[0]).astype(BF16)
    copies[2].wait()
    own[...] = mm(hot_own[...], local_rows[1]).astype(BF16)


def select_again_kernel(meta, hot_own, hot_other, rows, own, first, second):
    core = meta[1]
    half = first.shape[0]
    first[...] = mm(hot_other[:half, :], rows[1 - core]).astype(BF16)
    second[...] = mm(hot_other[half:, :], rows[1 - core]).astype(BF16)
    own[...] = mm(hot_own[...], rows[core]).astype(BF16)


def place_kernel(meta, hot_own, hot_other, rows, own, other, out):
    core = meta[1]
    for seq, hot, update in ((core, hot_own, own), (1 - core, hot_other, other)):
        out[seq] = (rows[seq].astype(F32) + mm_tn(hot[...], update[...])).astype(BF16)


def attend_kernel(
    meta, lengths, here, there, w_router, gain_attn, gain_mlp, w_query, w_key, w_value, w_out,
    up_own, up_other, chosen_out, normed_out, query_out, key_out, value_out, probs_out, mixed_out, attended_out,
    normed_mlp_out, rate_out, act_own, act_other, slope_own, slope_other, early_rows, late_rows, up_local, sem,
):
    copy = pltpu.make_async_copy(up_own, up_local, sem)
    copy.start()
    count = lengths[meta[1]] // 8
    slots, width = here.shape
    chosen = here[...].astype(F32) + there[...].astype(F32)
    chosen_out[...] = chosen.astype(BF16)
    score = jnp.sum(chosen * w_router[...].astype(F32), axis=-1, keepdims=True)
    rate = jax.nn.sigmoid(score)
    valid = lax.broadcasted_iota(jnp.int32, (slots, 1), 0) < count
    rate_out[...] = jnp.broadcast_to(jnp.where(valid, rate, 0.0), rate_out.shape)
    scale = lax.rsqrt(jnp.mean(chosen * chosen, axis=-1, keepdims=True) + EPS)
    normed = (chosen * scale * gain_attn[...]).astype(BF16)
    normed_out[...] = normed
    query_out[...] = mm(normed, w_query[...]).astype(BF16)
    key_out[...] = mm(normed, w_key[...]).astype(BF16)
    value_out[...] = mm(normed, w_value[...]).astype(BF16)
    head = width // NH
    pair = 2 * head
    i = lax.broadcasted_iota(jnp.int32, (slots, slots), 0)
    j = lax.broadcasted_iota(jnp.int32, (slots, slots), 1)
    allowed = (j <= i) & (j < count)
    first = lax.broadcasted_iota(jnp.int32, (slots, pair), 1) < head
    for p in range(NH // 2):
        cols = slice(p * pair, (p + 1) * pair)
        query = query_out[:, cols]
        keys = key_out[:, cols]
        values = value_out[:, cols]
        halves = []
        for h in range(2):
            mine = first if h == 0 else ~first
            logits = mm_nt(jnp.where(mine, query, jnp.zeros_like(query)), keys) * (head ** -0.5)
            logits = jnp.where(allowed, logits, -1e30)
            expd = jnp.exp(logits - jnp.max(logits, axis=-1, keepdims=True))
            probs = expd / jnp.sum(expd, axis=-1, keepdims=True)
            probs_out[2 * p + h] = probs
            halves.append(mm(probs.astype(BF16), values))
        mixed_out[:, cols] = jnp.where(first, halves[0], halves[1]).astype(BF16)
    attended = mm(mixed_out[...], w_out[...])
    attended_out[...] = attended
    hidden = chosen + attended
    scale = lax.rsqrt(jnp.mean(hidden * hidden, axis=-1, keepdims=True) + EPS)
    normed_mlp = (hidden * scale * gain_mlp[...]).astype(BF16)
    normed_mlp_out[...] = normed_mlp
    for w_up, act, slope in ((up_other, act_other, slope_other), (up_local, act_own, slope_own)):
        if w_up is up_local:
            copy.wait()
        up = mm(normed_mlp, w_up[...])
        square = up * up
        root = 0.7978845608028654
        t = jnp.tanh(root * (up + 0.044715 * (square * up)))
        act[...] = (0.5 * up * (1.0 + t)).astype(BF16)
        slope[...] = 0.5 * (1.0 + t) + (0.5 * root) * up * (1.0 - t * t) * (1.0 + 0.134145 * square)
    early_rows[:slots, :] = normed_out[...]
    early_rows[slots:, :] = mixed_out[...]
    late_rows[:slots, :] = normed_mlp
    late_rows[slots:, :] = act_other[...]


def mlp_kernel(
    rate, here, there, slope_own, slope_other, up_own, up_other, down_own, down_other,
    back_own, rows, grad_normed,
):
    seen = here[...].astype(F32) + there[...].astype(F32)
    moved = (rate[:, :1] * seen).astype(BF16)
    slots = moved.shape[0]
    rows[:slots, :] = moved
    total = None
    for w_up, w_down, slope, own in (
        (up_own, down_own, slope_own, True),
        (up_other, down_other, slope_other, False),
    ):
        grad_up = (mm_nt(moved, w_down[...]) * slope[...]).astype(BF16)
        if own:
            back_own[...] = grad_up
        else:
            rows[slots:, :] = grad_up
        part = mm_nt(grad_up, w_up[...])
        total = part if total is None else total + part
    grad_normed[...] = total.astype(BF16)


def moved_kernel(act_own, act_other, down_own, down_other, moved):
    moved[...] = (mm(act_own[...], down_own[...]) + mm(act_other[...], down_other[...])).astype(BF16)


def mlp_grads_kernel(whole, meta, act, back, late_rows, rows, late_got, got, *outs):
    slots, width = act.shape
    moved, moved_got = rows[:slots, :], got[:slots, :]
    back_got = got[slots:, :]
    if whole:
        outs[0][...] = mm_tn(act[...], moved) + mm_tn(late_got[slots:, :], moved_got)
        outs[1][...] = mm_tn(late_rows[:slots, :], back[...]) + mm_tn(late_got[:slots, :], back_got)
        return
    half = width // 2
    d_send, u_send, d_keep, u_keep = outs
    for bit, send in ((1, True), (0, False)):
        cols = pl.ds(pl.multiple_of((meta[Y] ^ bit) * half, 128), half)
        d = mm_tn(act[:, cols], moved) + mm_tn(late_got[slots:, cols], moved_got)
        cols = pl.ds(pl.multiple_of((meta[Z0] ^ bit) * half, 128), half)
        u = mm_tn(late_rows[:slots, cols], back[...]) + mm_tn(late_got[:slots, cols], back_got)
        if send:
            d_send[...] = d.astype(BF16)
            u_send[...] = u.astype(BF16)
        else:
            d_keep[...] = d
            u_keep[...] = u


def norm_back(values, gain, grad):
    scale = lax.rsqrt(jnp.mean(values * values, axis=-1, keepdims=True) + EPS)
    scaled = grad * gain
    inner = jnp.mean(scaled * values, axis=-1, keepdims=True)
    back = scale * scaled - values * (scale * scale * scale * inner)
    return back, jnp.sum(grad * values * scale, axis=0, keepdims=True)


def attend_back_kernel(
    chosen_in, attended, gain_attn, gain_mlp, gn_here, gn_there, rate, seen_here, seen_there,
    query_in, key_in, value_in, probs_in, w_query, w_key, w_value, w_out, meta,
    kept_rows, sent_rows, grad_sum, small, mixed_back, grad_query, grad_key, grad_value,
):
    small[...] = jnp.zeros_like(small)
    slots, width = chosen_in.shape
    head = width // NH
    pair = 2 * head
    chosen = chosen_in[...].astype(F32)
    grad_normed_mlp = gn_here[...].astype(F32) + gn_there[...].astype(F32)
    grad_hidden, gain_grad = norm_back(chosen + attended[...], gain_mlp[...], grad_normed_mlp)
    small[2:3, :] = gain_grad
    seen = seen_here[...].astype(F32) + seen_there[...].astype(F32)
    grad_attended = (rate[:, :1] * seen + grad_hidden).astype(BF16)
    mixed_back[...] = mm_nt(grad_attended, w_out[...]).astype(BF16)
    first = lax.broadcasted_iota(jnp.int32, (slots, pair), 1) < head
    factor = head ** -0.5
    for p in range(NH // 2):
        cols = slice(p * pair, (p + 1) * pair)
        query = query_in[:, cols]
        keys = key_in[:, cols]
        values = value_in[:, cols]
        back = mixed_back[:, cols]
        parts = []
        for h in range(2):
            mine = first if h == 0 else ~first
            probs = probs_in[2 * p + h]
            grad_probs = mm_nt(jnp.where(mine, back, jnp.zeros_like(back)), values)
            gv = mm_tn(probs.astype(BF16), back)
            inner = jnp.sum(grad_probs * probs, axis=-1, keepdims=True)
            grad_logits = (probs * (grad_probs - inner)).astype(BF16)
            gq = mm(grad_logits, keys) * factor
            gk = mm_tn(grad_logits, query) * factor
            parts.append((gq, gk, gv))
        for out, a, b in zip((grad_query, grad_key, grad_value), parts[0], parts[1]):
            out[:, cols] = jnp.where(first, a, b).astype(BF16)
    grad_normed = (
        mm_nt(grad_query[...], w_query[...])
        + mm_nt(grad_key[...], w_key[...])
        + mm_nt(grad_value[...], w_value[...])
    )
    back, gain_grad = norm_back(chosen, gain_attn[...], grad_normed)
    small[1:2, :] = gain_grad
    grad_sum[...] = back + grad_hidden
    for core, (low, high) in enumerate(((kept_rows, sent_rows), (sent_rows, kept_rows))):

        @pl.when(meta[1] == core)
        def _():
            low[:slots, :] = grad_query[...]
            low[slots:, :] = grad_key[...]
            high[:slots, :] = grad_value[...]
            high[slots:, :] = grad_attended


def attend_grads_kernel(whole, meta, *refs):
    if not whole:
        vectors, refs = refs[0], refs[1:]
    early_rows, early_got, mine, got, *outs, full = refs
    slots = mine.shape[0] // 2
    half = mine.shape[1] // 2
    cols = pl.ds(pl.multiple_of(meta[3] * half, 128), half)
    lower, upper = pl.ds(0, slots), pl.ds(slots, slots)
    second = pl.ds(pl.multiple_of(meta[1] * slots, slots), slots)
    full[:half, :] = mm_tn(early_rows[lower, cols], mine[lower, :]) + mm_tn(early_got[lower, cols], got[lower, :])
    full[half:, :] = mm_tn(early_rows[second, cols], mine[upper, :]) + mm_tn(early_got[second, cols], got[upper, :])
    if whole:
        outs[0][...] = full[...]
        return
    part = half // 2
    send_a, send_b, keep_a, keep_b, out = outs
    for at, bit, send, keep in ((0, Y, send_a, keep_a), (half, Z0, send_b, keep_b)):
        yours = pl.multiple_of(at + (1 - meta[bit]) * part, part)
        send[:part, :] = full[pl.ds(yours, part), :].astype(BF16)
        keep[...] = full[pl.ds(pl.multiple_of(at + meta[bit] * part, part), part), :]
    out[...] = vectors[...]
    send_a[part:, :] = split_vectors(vectors[...]).astype(BF16)


def slots_kernel(
    chosen_in, attended, rate_in, seen_here, seen_there, moved_here, moved_there, w_router, grad_sum,
    small, update, grad_chosen, vectors,
):
    chosen = chosen_in[...].astype(F32)
    rate = rate_in[:, :1]
    seen = seen_here[...].astype(F32) + seen_there[...].astype(F32)
    delta = attended[...] + (moved_here[...].astype(F32) + moved_there[...].astype(F32))
    update[...] = (rate * delta).astype(BF16)
    score = rate * (1.0 - rate) * jnp.sum(seen * delta, axis=-1, keepdims=True)
    grad_chosen[...] = (grad_sum[...] + score * w_router[...].astype(F32)).astype(BF16)
    vectors[...] = jnp.zeros_like(vectors)
    vectors[0:1, :] = jnp.sum(score * chosen, axis=0, keepdims=True)
    vectors[1:3, :] = small[1:3, :]


def reduce_kernel(plan, gots, sends, meta, *refs):
    keeps, refs = refs[: len(plan)], refs[len(plan) :]
    got, refs = refs[:gots], refs[gots:]
    send, kept = refs[:sends], refs[sends:]
    for keep, new, (rows, bit, g, g_row, t, t_row) in zip(keeps, kept, plan):
        half = rows // 2
        mine = pl.multiple_of(meta[bit] * half, half)
        yours = pl.multiple_of((1 - meta[bit]) * half, half)
        send[t][t_row : t_row + half, :] = (
            keep[pl.ds(yours, half), :] + got[g][pl.ds(g_row + yours, half), :].astype(F32)
        ).astype(BF16)
        new[...] = keep[pl.ds(mine, half), :] + got[g][pl.ds(g_row + mine, half), :].astype(F32)


def split_vectors(v):
    high = v.astype(BF16).astype(F32)
    return jnp.concatenate([high, (v - high).astype(BF16).astype(F32)], axis=0)


def join_vectors(v):
    return v[:8, :] + v[8:, :]


def reduce_small_kernel(plan, gots, sends, meta, *refs):
    vectors, refs = refs[0], refs[1:]
    out = refs[-1]
    reduce_kernel(plan, gots, sends, meta, *refs[:-1])
    got = refs[len(plan)]
    own = join_vectors(split_vectors(vectors[...])) + join_vectors(got[got.shape[0] - 16 :, :].astype(F32))
    out[...] = own
    send = refs[len(plan) + gots]
    send[send.shape[0] - 16 :, :] = split_vectors(own).astype(BF16)


def round_kernel(keep, got, cur):
    cur[...] = (keep[...] + got[...].astype(F32)).astype(BF16)


def round_both_kernel(vectors, first, second, got_first, got_second, cur, out):
    rows = first.shape[0]
    cur[:rows, :] = (first[...] + got_first[:rows, :].astype(F32)).astype(BF16)
    cur[rows : 2 * rows, :] = (second[...] + got_second[...].astype(F32)).astype(BF16)
    own = join_vectors(split_vectors(vectors[...])) + join_vectors(got_first[rows:, :].astype(F32))
    cur[2 * rows :, :] = split_vectors(own).astype(BF16)
    out[...] = own


def last_kernel(cur, got, out):
    out[...] = (cur[...].astype(F32) + got[...].astype(F32)).astype(BF16)


def last_both_kernel(vectors, cur, got, first, second, both, *outs):
    rows = first.shape[0]
    for at, out in ((0, first), (rows, second)):
        out[...] = (cur[at : at + rows, :].astype(F32) + got[at : at + rows, :].astype(F32)).astype(BF16)
        both[at : at + rows, :] = out[...]
    own = join_vectors(split_vectors(vectors[...])) + join_vectors(got[2 * rows :, :].astype(F32))
    for n, out in enumerate(outs):
        out[...] = own[n, :]


def join_kernel(plan, meta, *refs):
    count = len(plan)
    for (rows, bit, row, got_row), own, got, out in zip(
        plan, refs[:count], refs[count : 2 * count], refs[2 * count :]
    ):
        mine = pl.multiple_of(meta[bit] * rows, rows)
        yours = pl.multiple_of((1 - meta[bit]) * rows, rows)
        out[pl.ds(mine, rows), :] = own[row : row + rows, :].astype(out.dtype)
        out[pl.ds(yours, rows), :] = got[got_row : got_row + rows, :].astype(out.dtype)


def join_both_kernel(meta, own_a, own_b, got_a, got_b, out_a, out_b, both, far):
    rows = own_a.shape[0]
    for n, bit, own, got, out in ((0, Z0, own_a, got_a, out_a), (1, Y, own_b, got_b, out_b)):
        mine = pl.multiple_of(meta[bit] * rows, rows)
        yours = pl.multiple_of((1 - meta[bit]) * rows, rows)
        out[pl.ds(mine, rows), :] = own[...]
        out[pl.ds(yours, rows), :] = got[...]
        both[2 * n * rows : 2 * (n + 1) * rows, :] = out[...]
        far[n * rows : (n + 1) * rows, :] = got[...]


def stack_kernel(got_a, got_b, late):
    rows = got_a.shape[0]
    late[:rows, :] = got_a[...]
    late[rows:, :] = got_b[...]


def attention_kernel(far, meta, *refs):
    outs, (block, sems) = refs[-6:-2], refs[-2:]
    count = 3 if far else 2
    core, side = meta[1], meta[3] ^ far
    part = block.shape[1] // 2
    at = pl.multiple_of(side * 2 * part, 8)
    for other in range(2):
        pieces = refs[other * count : (other + 1) * count]
        for packet, bit, inner in ((0, meta[Y], meta[Z0]), (1, meta[Z0], meta[Y])):
            m = 2 * (core ^ other) + packet
            rows = slice(packet * part, (packet + 1) * part)
            if far:
                size = part // 2
                for n in range(2):
                    start = pl.multiple_of(bit * part + (inner ^ n) * size, 8)
                    block[m, pl.ds(start, size), :] = pieces[n][packet * size : (packet + 1) * size, :].astype(F32)
            else:
                block[m, pl.ds(pl.multiple_of(bit * part, 8), part), :] = pieces[0][rows, :].astype(F32)
            block[m, pl.ds(pl.multiple_of((1 - bit) * part, 8), part), :] = pieces[-1][rows, :].astype(F32)
            for n, out in enumerate(outs):

                @pl.when(m == n)
                def _():
                    pltpu.make_async_copy(block.at[n], out.at[pl.ds(at, 2 * part), :], sems.at[n]).start()

    for n, out in enumerate(outs):
        pltpu.make_async_copy(block.at[n], out.at[pl.ds(at, 2 * part), :], sems.at[n]).wait()


def attention_near_kernel(*refs):
    attention_kernel(0, *refs)


def attention_far_kernel(*refs):
    attention_kernel(1, *refs)


def swap(v, axis, size, bits):
    return lax.ppermute(v, axis, [(i, i ^ bits) for i in range(size)])


def body(
    batch, tokens, lengths, picks, w_router, gain_attn, gain_mlp, w_query, w_key, w_value, w_out,
    w_up, w_down, cotangent,
):
    place, index = lax.axis_index("seq"), lax.axis_index("batch")
    core, side = place % 2, place // 2
    seqs, length, width = tokens.shape
    local = picks.shape[1]
    slots = 4 * local
    n, half = width, width // 2
    hidden_units = w_up.shape[1]
    across = functools.partial(swap, axis="seq", size=4)
    along = lambda v, bit: swap(v, "batch", batch, 1 << bit)
    row = lambda v: v.reshape(1, width)
    gain_attn, gain_mlp, w_router = row(gain_attn), row(gain_mlp), row(w_router)
    meta = jnp.stack(
        [place, core, index, side] + [place ^ k for k in range(4)] + [(index >> k) & 1 for k in range(3)]
    ).astype(jnp.int32)
    rows = lambda count: ((count, width), BF16)
    wide = lambda count: ((count, width), F32)
    hot = ((slots, length), BF16)
    act = ((slots, hidden_units), BF16)
    slope = ((slots, hidden_units), F32)

    got = [across(picks, bits=k) for k in (1, 2, 3)]
    own, other, hot_own, hot_other = call(
        "SE", select_kernel, [meta, *got, picks, tokens], [rows(slots)] * 2 + [hot] * 2,
        specs=[SMEM] + [VMEM] * 3 + [HBM] * 2,
        scratch=[
            pltpu.VMEM((2, length, width), BF16), pltpu.VMEM(picks.shape, jnp.int32),
            pltpu.SemaphoreType.DMA((3,)),
        ],
        vmem=52,
    )
    up_other, down_other = across(w_up, bits=1), across(w_down, bits=1)
    here = own + across(other, bits=1)
    there = across(here, bits=2)
    own, *other = call(
        "SA", select_again_kernel, [meta, hot_own, hot_other, cotangent], [rows(slots)] + [rows(slots // 2)] * 2,
        specs=[SMEM] + [VMEM] * 3,
    )
    seen_here = own + jnp.concatenate([across(v, bits=1) for v in other], axis=0)
    seen_there = across(seen_here, bits=2)

    (
        chosen, normed, query, keys, values, probs, mixed, attended, normed_mlp, rate,
        act_own, act_other, slope_own, slope_other, early_rows, late_rows,
    ) = call(
        "AT", attend_kernel,
        [meta, lengths, here, there, w_router, gain_attn, gain_mlp, w_query, w_key, w_value, w_out, w_up, up_other],
        [rows(slots)] * 5 + [((NH, slots, slots), F32), rows(slots), wide(slots), rows(slots), ((slots, 128), F32)]
        + [act] * 2 + [slope] * 2 + [rows(2 * slots)] * 2,
        specs=[SMEM] * 2 + [VMEM] * 9 + [HBM, VMEM], after=[seen_here],
        scratch=[pltpu.VMEM(w_up.shape, BF16), pltpu.SemaphoreType.DMA],
    )
    early_got, late_got = across(early_rows, bits=1), across(late_rows, bits=1)
    back_own, moved_rows, gn_here = call(
        "ML", mlp_kernel,
        [rate, seen_here, seen_there, slope_own, slope_other, w_up, up_other, w_down, down_other],
        [act, rows(2 * slots), rows(slots)],
    )
    gn_there = across(gn_here, bits=2)
    moved_got = across(moved_rows, bits=1)
    moved_here = call("MV", moved_kernel, [act_own, act_other, w_down, down_other], [rows(slots)], after=[gn_here])[0]
    moved_there = across(moved_here, bits=2)

    def mlp_grads(outs, after):
        return call(
            "F", functools.partial(mlp_grads_kernel, len(outs) == 2),
            [meta, act_own, back_own, late_rows, moved_rows, late_got, moved_got], outs,
            specs=[SMEM] + [VMEM] * 6, after=after,
        )

    def attend_back(after):
        return call(
            "AB", attend_back_kernel,
            [
                chosen, attended, gain_attn, gain_mlp, gn_here, gn_there, rate, seen_here, seen_there,
                query, keys, values, probs, w_query, w_key, w_value, w_out, meta,
            ],
            [rows(2 * slots)] * 2 + [wide(slots), wide(8)], specs=[VMEM] * 17 + [SMEM],
            scratch=[pltpu.VMEM((slots, width), BF16)] * 4, after=after,
        )

    def attend_grads(mine, got, vectors, outs, after):
        more = [] if vectors is None else [vectors]
        return call(
            "FA", functools.partial(attend_grads_kernel, vectors is None),
            [meta, *more, early_rows, early_got, mine, got], outs,
            specs=[SMEM] + [VMEM] * (4 + len(more)), scratch=[pltpu.VMEM((width, width), F32)], after=after,
        )

    def slot_sums(grad_sum, small, after):
        update, grad_chosen, vectors = call(
            "SL", slots_kernel,
            [chosen, attended, rate, seen_here, seen_there, moved_here, moved_there, w_router, grad_sum, small],
            [rows(slots), rows(slots), wide(8)], after=after,
        )
        return update, grad_chosen, vectors + across(vectors, bits=1)

    def placed(tag, values, mine, core, after=()):
        return call(
            tag, place_kernel, [meta, hot_own, hot_other, values, mine, core],
            [(values.shape, BF16)], specs=[SMEM] + [VMEM] * 5, after=after, token=True,
        )

    if batch != 8:
        whole = ((width, width), F32)
        down, up = mlp_grads([whole] * 2, [])
        mine, theirs, grad_sum, small = attend_back([])
        update, grad_chosen, vectors = slot_sums(grad_sum, small, [])
        attention = attend_grads(mine, across(theirs, bits=1), None, [whole], [])[0]
        down, up, attention, vectors = lax.psum((down, up, attention, vectors), "batch")
        attention = lax.all_gather(attention, "seq").reshape(2, 2, 2, half, width)
        return (
            placed("P1", tokens, update, across(update, bits=1))[0],
            placed("P2", cotangent, grad_chosen, across(grad_chosen, bits=1))[0],
            vectors[0], vectors[1], vectors[2],
            *(attention[:, m // 2, m % 2].reshape(width, width) for m in range(4)), up, down,
        )

    def reduce(tag, keeps, gots, plan, sends, after=(), vectors=None):
        kernel = functools.partial(reduce_kernel, plan, len(gots), len(sends))
        outs = [rows(count) for count in sends] + [wide(p[0] // 2) for p in plan]
        ins = [meta, *keeps, *gots]
        if vectors is not None:
            kernel = functools.partial(reduce_small_kernel, plan, len(gots), len(sends))
            ins = [meta, vectors, *keeps, *gots]
            outs.append(wide(8))
        return call(tag, kernel, ins, outs, specs=[SMEM] + [VMEM] * (len(ins) - 1), after=after)

    def join(tag, bit, own, got, dtype=BF16, after=(), token=False):
        count = own.shape[0]
        return call(
            tag, functools.partial(join_kernel, [(count, bit, 0, 0)]), [meta, own, got],
            [((2 * count, width), dtype)], specs=[SMEM] + [VMEM] * 2, after=after, token=token,
        )

    def attention(tag, kernel, pieces, outs=(), after=()):
        return call(
            tag, kernel, [meta, *pieces, *outs], [wide(width)] * 4,
            specs=[SMEM] + [VMEM] * len(pieces) + [HBM] * len(outs), out_specs=[HBM] * 4,
            scratch=[pltpu.VMEM((4, half, width), F32), pltpu.SemaphoreType.DMA((4,))],
            aliases={1 + len(pieces) + m: m for m in range(len(outs))}, after=after, token=True,
        )

    v, moved = {}, {}

    def kept(name, value):
        moved[name] = value
        return value

    moved["M"] = moved_there

    def step_f(after):
        d, u, v["d_keep"], v["u_keep"] = mlp_grads([rows(half)] * 2 + [wide(half)] * 2, after)
        v["d"], v["u"] = kept("d1", along(d, 0)), kept("u1", along(u, 1))
        return v["d_keep"]

    def step_ab(after):
        v["mine"], theirs, v["sum"], v["small"] = attend_back(after)
        v["got"] = kept("th", across(theirs, bits=1))
        return v["small"]

    def step_sl(after):
        v["update"], v["grad_chosen"], v["vectors"] = slot_sums(v["sum"], v["small"], after)
        v["update_core"] = kept("up", across(v["update"], bits=1))
        v["chosen_core"] = kept("gc", across(v["grad_chosen"], bits=1))
        return v["update"]

    def step_fa(after):
        a, b, v["a_keep"], v["b_keep"], v["vectors"] = attend_grads(
            v["mine"], v["got"], v["vectors"],
            [rows(half // 2 + 16), rows(half // 2), wide(half // 2), wide(half // 2), wide(8)], after,
        )
        v["a"], v["b"] = kept("a1", along(a, 0)), kept("b1", along(b, 1))
        return v["a_keep"]

    def step_r2(after):
        send, v["d_keep"] = reduce("R2", [v["d_keep"]], [v["d"]], [(n // 2, Z0, 0, 0, 0, 0)], [n // 4], after)
        v["d"] = kept("d2", along(send, 1))
        return v["d_keep"]

    def step_r2u(after):
        send, v["u_keep"] = reduce("R2U", [v["u_keep"]], [v["u"]], [(n // 2, Y, 0, 0, 0, 0)], [n // 4], after)
        v["u"] = kept("u2", along(send, 0))
        return v["u_keep"]

    def step_a2(after):
        a, b, v["a_keep"], v["b_keep"], v["vectors"] = reduce(
            "A2", [v["a_keep"], v["b_keep"]], [v["a"], v["b"]],
            [(half // 2, Z0, 0, 0, 0, 0), (half // 2, Y, 1, 0, 1, 0)],
            [half // 4 + 16, half // 4], after, v["vectors"],
        )
        v["a"], v["b"] = kept("a2", along(a, 1)), kept("b2", along(b, 0))
        return v["a_keep"]

    def third(tag, key):
        def step(after):
            v[key + "_cur"] = call(tag, round_kernel, [v[key + "_keep"], v[key]], [rows(n // 4)], after=after)[0]
            v[key] = kept(key + "3", along(v[key + "_cur"], 2))
            return v[key + "_cur"]

        return step

    def step_a3(after):
        v["ab_cur"], v["vectors"] = call(
            "A3", round_both_kernel, [v["vectors"], v["a_keep"], v["b_keep"], v["a"], v["b"]],
            [rows(half // 2 + 16), wide(8)], after=after,
        )
        v["ab"] = kept("ab3", along(v["ab_cur"], 2))
        return v["vectors"]

    def fourth(tag, key, bit):
        def step(after):
            v[key + "_all"] = call(tag, last_kernel, [v[key + "_cur"], v[key]], [rows(n // 4)], after=after)[0]
            v[key] = kept(key + "5", along(v[key + "_all"], bit))
            return v[key + "_all"]

        return step

    def step_a4(after):
        v["a_all"], v["b_all"], near, *v["vectors"] = call(
            "A4", last_both_kernel, [v["vectors"], v["ab_cur"], v["ab"]],
            [rows(half // 4)] * 2 + [rows(half // 2)] + [((width,), F32)] * 3, after=after,
        )
        v["a"], v["b"] = kept("a5", along(v["a_all"], 1)), kept("b5", along(v["b_all"], 0))
        v["near"] = kept("x1", across(near, bits=2))
        return v["a_all"]

    def step_a5(after):
        a, b, v["early"], far = call(
            "A5", join_both_kernel, [meta, v["a_all"], v["b_all"], v["a"], v["b"]],
            [rows(half // 2)] * 2 + [rows(half), rows(half // 2)], specs=[SMEM] + [VMEM] * 4, after=after,
        )
        v["a"], v["b"] = kept("a6", along(a, 0)), kept("b6", along(b, 1))
        v["far"] = kept("x2", across(far, bits=2))
        v["early_core"] = kept("ce", across(v["early"], bits=1))
        return v["early"]

    def step_a6(after):
        v["late"] = call("A6", stack_kernel, [v["a"], v["b"]], [rows(half)], after=after)[0]
        v["side"] = kept("xl", across(v["late"], bits=2))
        v["late_core"] = kept("cl", across(v["late"], bits=1))
        return v["late"]

    def fifth(tag, key, bit, along_bit):
        def step(after):
            v[key + "_all"] = join(tag, bit, v[key + "_all"], v[key], after=after)[0]
            v[key] = kept(key + "6", along(v[key + "_all"], along_bit))
            return v[key + "_all"]

        return step

    def sixth(tag, key, bit):
        def step(after):
            v["grad_" + key], token = join(tag, bit, v[key + "_all"], v[key], F32, after, token=True)
            return token

        return step

    def place(tag, name, values, mine, core):
        def step(after):
            v[name], token = placed(tag, values, v[mine], v[core], after)
            return token

        return step

    def step_at0(after):
        *v["grads"], token = attention(
            "AT0", attention_near_kernel, [v["early"], v["late"], v["early_core"], v["late_core"]], after=after
        )
        return token

    def step_xc(after):
        side, *_ = lax.optimization_barrier((v["side"], *after))
        v["pieces"] = [v["near"], v["far"], side]
        v["pieces"] += [across(piece, bits=1) for piece in v["pieces"]]
        return after[0]

    def step_at1(after):
        *v["grads"], token = attention("AT1", attention_far_kernel, v["pieces"], v["grads"], after)
        return token

    steps = dict(
        F=step_f, AB=step_ab, SL=step_sl, FA=step_fa, R2=step_r2, R2U=step_r2u, A2=step_a2, A3=step_a3,
        D3=third("D3", "d"), U3=third("U3", "u"), D4=fourth("D4", "d", 1), U4=fourth("U4", "u", 0), A4=step_a4,
        A5=step_a5, A6=step_a6, D5=fifth("D5", "d", Z0, 0), U5=fifth("U5", "u", Y, 1), DU=sixth("DU", "d", Y),
        UU=sixth("UU", "u", Z0), P1=place("P1", "output", tokens, "update", "update_core"),
        P2=place("P2", "grad_tokens", cotangent, "grad_chosen", "chosen_core"), AT0=step_at0, XC=step_xc, AT1=step_at1,
    )
    after = [moved_here]
    for name in ORDER:
        after = [steps[name](after + [moved[key] for key in HOLD.get(name, ())])]
    return (
        v["output"], v["grad_tokens"], *v["vectors"], *v["grads"], v["grad_u"], v["grad_d"],
    )


def solution(mesh):
    rows, whole = P("batch", "seq", None), P()
    return jax.shard_map(
        functools.partial(body, mesh.shape["batch"]),
        mesh=mesh,
        in_specs=(
            rows, P("batch"), P("batch", "seq"), whole, whole, whole, whole, whole, whole, whole,
            P(None, "seq"), P("seq", None), rows,
        ),
        out_specs=(
            rows, rows, whole, whole, whole, whole, whole, whole, whole,
            P(None, "seq"), P("seq", None),
        ),
        check_vma=False,
    )
```

```python
import functools

import jax
import jax.numpy as jnp
from jax import lax
from jax.experimental import pallas as pl
from jax.experimental.pallas import tpu as pltpu
from jax.sharding import PartitionSpec as P

NH = 12
Y, Z0, Z1 = 8, 9, 10
ORDER = ("F", "AB", "MV", "R2", "FA", "SL", "D3", "A2", "A3", "D4", "R2U", "P2", "U3", "A4", "P1", "A5", "U4", "A6", "U5", "D5", "AT0", "UH", "XE", "DH", "ATE", "XC", "UU", "DU", "ATL")
WORK = {"P1": 1000, "D5": 600, "U5": 8000, "U4": 2000, "D3": 100, "SL": 1000, "UU": 100, "DU": 4000, "P2": 100, "R2": 4000, "AT0": 4000, "A6": 300, "A4": 1000, "A2": 300, "A3": 1000, "AT": 600, "ATE": 100, "R2U": 600, "ATL": 8000, "ML": 4000, "F": 300, "A5": 100, "D4": 300, "SE": 8000, "MV": 4000, "SA": 300}
HOLD = {"U5": ["x1"], "U3": ["d5"], "R2": ["u1"], "D4": ["up"]}
EPS = 1e-06
F32 = jnp.float32
BF16 = jnp.bfloat16
VMEM = pl.BlockSpec(memory_space=pltpu.VMEM)
SMEM = pl.BlockSpec(memory_space=pltpu.SMEM)
ANY = pl.BlockSpec(memory_space=pl.ANY)
HBM = pl.BlockSpec(memory_space=pltpu.HBM)


def mm(a, b):
    return jnp.dot(a, b, preferred_element_type=F32)


def mm_nt(a, b):
    return lax.dot_general(a, b, (((1,), (1,)), ((), ())), preferred_element_type=F32)


def mm_tn(a, b):
    return lax.dot_general(a, b, (((0,), (0,)), ((), ())), preferred_element_type=F32)


def call(
    tag, kernel, ins, outs, specs=None, scratch=(), vmem=12, after=(), name=None, token=False,
    out_specs=None, aliases=None,
):
    shapes = [jax.ShapeDtypeStruct(shape, dtype) for shape, dtype in outs]
    results = len(shapes)
    out_specs = list(out_specs or [VMEM] * results)
    if token:
        shapes.append(jax.ShapeDtypeStruct((8, 128), F32))
        out_specs.append(VMEM)
    count, extra = len(ins), len(after)

    def run(*refs):
        rest = refs[count + extra :]
        if token:
            rest[results][...] = jnp.zeros((8, 128), F32)
            rest = rest[:results] + rest[results + 1 :]
        kernel(*refs[:count], *rest)

    return pl.pallas_call(
        run,
        out_shape=tuple(shapes),
        in_specs=(specs or [VMEM] * count) + [ANY] * extra,
        out_specs=tuple(out_specs),
        scratch_shapes=list(scratch),
        input_output_aliases=aliases or {},
        name=name or getattr(kernel, "func", kernel).__name__,
        cost_estimate=pl.CostEstimate(flops=1 + WORK.get(tag, 0) * 1_000_000, bytes_accessed=1, transcendentals=0),
        compiler_params=pltpu.CompilerParams(vmem_limit_bytes=vmem * 1024 * 1024),
    )(*ins, *after)


def select_kernel(meta, p1, p2, p3, picks, rows, own, other, hot_own, hot_other, local_rows, p0, sems):
    core = meta[1]
    copies = [
        pltpu.make_async_copy(picks, p0, sems.at[0]),
        pltpu.make_async_copy(rows.at[1 - core], local_rows.at[0], sems.at[1]),
        pltpu.make_async_copy(rows.at[core], local_rows.at[1], sems.at[2]),
    ]
    for copy in copies:
        copy.start()
    length = rows.shape[1]
    local = p1.shape[1]
    base = meta[0] * length
    down = lax.broadcasted_iota(jnp.int32, (local, local), 0)
    along = lax.broadcasted_iota(jnp.int32, (local, local), 1)
    places = lax.broadcasted_iota(jnp.int32, (local, length), 1)
    for k, part in ((1, p1), (2, p2), (3, p3), (0, p0)):
        if k == 0:
            copies[0].wait()
        at = pl.multiple_of(meta[4 + k] * local, local)
        for seq, hot in ((1 - core, hot_other), (core, hot_own)):
            row = part[pl.ds(seq, 1), :]
            column = jnp.sum(jnp.where(down == along, row, 0), axis=1, keepdims=True)
            hot[pl.ds(at, local), :] = jnp.where(column - base == places, 1.0, 0.0).astype(BF16)
    copies[1].wait()
    other[...] = mm(hot_other[...], local_rows[0]).astype(BF16)
    copies[2].wait()
    own[...] = mm(hot_own[...], local_rows[1]).astype(BF16)


def select_again_kernel(meta, hot_own, hot_other, rows, own, first, second):
    core = meta[1]
    half = first.shape[0]
    first[...] = mm(hot_other[:half, :], rows[1 - core]).astype(BF16)
    second[...] = mm(hot_other[half:, :], rows[1 - core]).astype(BF16)
    own[...] = mm(hot_own[...], rows[core]).astype(BF16)


def place_kernel(meta, hot_own, hot_other, rows, own, other, out):
    core = meta[1]
    for seq, hot, update in ((core, hot_own, own), (1 - core, hot_other, other)):
        out[seq] = (rows[seq].astype(F32) + mm_tn(hot[...], update[...])).astype(BF16)


def attend_kernel(
    meta, lengths, here, there, w_router, gain_attn, gain_mlp, w_query, w_key, w_value, w_out,
    up_own, up_other, chosen_out, normed_out, query_out, key_out, value_out, probs_out, mixed_out, attended_out,
    normed_mlp_out, rate_out, act_own, act_other, slope_own, slope_other, early_rows, late_rows, up_local, sem,
):
    copy = pltpu.make_async_copy(up_own, up_local, sem)
    copy.start()
    count = lengths[meta[1]] // 8
    slots, width = here.shape
    chosen = here[...].astype(F32) + there[...].astype(F32)
    chosen_out[...] = chosen.astype(BF16)
    score = jnp.sum(chosen * w_router[...].astype(F32), axis=-1, keepdims=True)
    rate = jax.nn.sigmoid(score)
    valid = lax.broadcasted_iota(jnp.int32, (slots, 1), 0) < count
    rate_out[...] = jnp.broadcast_to(jnp.where(valid, rate, 0.0), rate_out.shape)
    scale = lax.rsqrt(jnp.mean(chosen * chosen, axis=-1, keepdims=True) + EPS)
    normed = (chosen * scale * gain_attn[...]).astype(BF16)
    normed_out[...] = normed
    query_out[...] = mm(normed, w_query[...]).astype(BF16)
    key_out[...] = mm(normed, w_key[...]).astype(BF16)
    value_out[...] = mm(normed, w_value[...]).astype(BF16)
    head = width // NH
    pair = 2 * head
    i = lax.broadcasted_iota(jnp.int32, (slots, slots), 0)
    j = lax.broadcasted_iota(jnp.int32, (slots, slots), 1)
    allowed = (j <= i) & (j < count)
    first = lax.broadcasted_iota(jnp.int32, (slots, pair), 1) < head
    for p in range(NH // 2):
        cols = slice(p * pair, (p + 1) * pair)
        query = query_out[:, cols]
        keys = key_out[:, cols]
        values = value_out[:, cols]
        halves = []
        for h in range(2):
            mine = first if h == 0 else ~first
            logits = mm_nt(jnp.where(mine, query, jnp.zeros_like(query)), keys) * (head ** -0.5)
            logits = jnp.where(allowed, logits, -1e30)
            expd = jnp.exp(logits - jnp.max(logits, axis=-1, keepdims=True))
            probs = expd / jnp.sum(expd, axis=-1, keepdims=True)
            probs_out[2 * p + h] = probs
            halves.append(mm(probs.astype(BF16), values))
        mixed_out[:, cols] = jnp.where(first, halves[0], halves[1]).astype(BF16)
    attended = mm(mixed_out[...], w_out[...])
    attended_out[...] = attended
    hidden = chosen + attended
    scale = lax.rsqrt(jnp.mean(hidden * hidden, axis=-1, keepdims=True) + EPS)
    normed_mlp = (hidden * scale * gain_mlp[...]).astype(BF16)
    normed_mlp_out[...] = normed_mlp
    for w_up, act, slope in ((up_other, act_other, slope_other), (up_local, act_own, slope_own)):
        if w_up is up_local:
            copy.wait()
        up = mm(normed_mlp, w_up[...])
        square = up * up
        root = 0.7978845608028654
        t = jnp.tanh(root * (up + 0.044715 * (square * up)))
        act[...] = (0.5 * up * (1.0 + t)).astype(BF16)
        slope[...] = 0.5 * (1.0 + t) + (0.5 * root) * up * (1.0 - t * t) * (1.0 + 0.134145 * square)
    early_rows[:slots, :] = normed_out[...]
    early_rows[slots:, :] = mixed_out[...]
    late_rows[:slots, :] = normed_mlp
    late_rows[slots:, :] = act_other[...]


def mlp_kernel(
    rate, here, there, slope_own, slope_other, up_own, up_other, down_own, down_other,
    back_own, rows, grad_normed,
):
    seen = here[...].astype(F32) + there[...].astype(F32)
    moved = (rate[:, :1] * seen).astype(BF16)
    slots = moved.shape[0]
    rows[:slots, :] = moved
    total = None
    for w_up, w_down, slope, own in (
        (up_own, down_own, slope_own, True),
        (up_other, down_other, slope_other, False),
    ):
        grad_up = (mm_nt(moved, w_down[...]) * slope[...]).astype(BF16)
        if own:
            back_own[...] = grad_up
        else:
            rows[slots:, :] = grad_up
        part = mm_nt(grad_up, w_up[...])
        total = part if total is None else total + part
    grad_normed[...] = total.astype(BF16)


def moved_kernel(act_own, act_other, down_own, down_other, moved):
    moved[...] = (mm(act_own[...], down_own[...]) + mm(act_other[...], down_other[...])).astype(BF16)


def mlp_grads_kernel(whole, meta, act, back, late_rows, rows, late_got, got, *outs):
    slots, width = act.shape
    moved, moved_got = rows[:slots, :], got[:slots, :]
    back_got = got[slots:, :]
    if whole:
        outs[0][...] = mm_tn(act[...], moved) + mm_tn(late_got[slots:, :], moved_got)
        outs[1][...] = mm_tn(late_rows[:slots, :], back[...]) + mm_tn(late_got[:slots, :], back_got)
        return
    half = width // 2
    d_send, u_send, d_keep, u_keep = outs
    for bit, send in ((1, True), (0, False)):
        cols = pl.ds(pl.multiple_of((meta[Y] ^ bit) * half, 128), half)
        d = mm_tn(act[:, cols], moved) + mm_tn(late_got[slots:, cols], moved_got)
        cols = pl.ds(pl.multiple_of((meta[Z0] ^ bit) * half, 128), half)
        u = mm_tn(late_rows[:slots, cols], back[...]) + mm_tn(late_got[:slots, cols], back_got)
        if send:
            d_send[...] = d.astype(BF16)
            u_send[...] = u.astype(BF16)
        else:
            d_keep[...] = d
            u_keep[...] = u


def norm_back(values, gain, grad):
    scale = lax.rsqrt(jnp.mean(values * values, axis=-1, keepdims=True) + EPS)
    scaled = grad * gain
    inner = jnp.mean(scaled * values, axis=-1, keepdims=True)
    back = scale * scaled - values * (scale * scale * scale * inner)
    return back, jnp.sum(grad * values * scale, axis=0, keepdims=True)


def attend_back_kernel(
    chosen_in, attended, gain_mlp, gn_here, gn_there, rate, seen_here, seen_there,
    query_in, key_in, value_in, probs_in, w_out, meta,
    kept_rows, sent_rows, grad_query, grad_key, grad_value, hidden_out, small, mixed_back,
):
    small[...] = jnp.zeros_like(small)
    slots, width = chosen_in.shape
    head = width // NH
    pair = 2 * head
    chosen = chosen_in[...].astype(F32)
    grad_normed_mlp = gn_here[...].astype(F32) + gn_there[...].astype(F32)
    grad_hidden, gain_grad = norm_back(chosen + attended[...], gain_mlp[...], grad_normed_mlp)
    small[2:3, :] = gain_grad
    hidden_out[...] = grad_hidden
    seen = seen_here[...].astype(F32) + seen_there[...].astype(F32)
    grad_attended = (rate[:, :1] * seen + grad_hidden).astype(BF16)
    mixed_back[...] = mm_nt(grad_attended, w_out[...]).astype(BF16)
    first = lax.broadcasted_iota(jnp.int32, (slots, pair), 1) < head
    factor = head ** -0.5
    for p in range(NH // 2):
        cols = slice(p * pair, (p + 1) * pair)
        query = query_in[:, cols]
        keys = key_in[:, cols]
        values = value_in[:, cols]
        back = mixed_back[:, cols]
        back_turned, query_turned = back.T, query.T
        for_query, for_key, for_value = [], [], []
        for h in range(2):
            mine = first if h == 0 else ~first
            rows = slice(h * head, (h + 1) * head)
            probs = probs_in[2 * p + h]
            grad_probs = mm_nt(jnp.where(mine, back, jnp.zeros_like(back)), values)
            for_value.append(mm(back_turned[rows, :], probs.astype(BF16)))
            inner = jnp.sum(grad_probs * probs, axis=-1, keepdims=True)
            grad_logits = (probs * (grad_probs - inner)).astype(BF16)
            for_query.append(mm(grad_logits, keys) * factor)
            for_key.append(mm(query_turned[rows, :], grad_logits) * factor)
        grad_query[:, cols] = jnp.where(first, for_query[0], for_query[1]).astype(BF16)
        grad_key[:, cols] = jnp.concatenate(for_key, axis=0).astype(BF16).T
        grad_value[:, cols] = jnp.concatenate(for_value, axis=0).astype(BF16).T
    for core, (low, high) in enumerate(((kept_rows, sent_rows), (sent_rows, kept_rows))):

        @pl.when(meta[1] == core)
        def _():
            low[:slots, :] = grad_query[...]
            low[slots:, :] = grad_key[...]
            high[:slots, :] = grad_value[...]
            high[slots:, :] = grad_attended


def attend_grads_kernel(whole, meta, *refs):
    early_rows, early_got, mine, got, *outs, full = refs
    slots = mine.shape[0] // 2
    half = mine.shape[1] // 2
    cols = pl.ds(pl.multiple_of(meta[3] * half, 128), half)
    lower, upper = pl.ds(0, slots), pl.ds(slots, slots)
    second = pl.ds(pl.multiple_of(meta[1] * slots, slots), slots)
    full[:half, :] = mm_tn(early_rows[lower, cols], mine[lower, :]) + mm_tn(early_got[lower, cols], got[lower, :])
    full[half:, :] = mm_tn(early_rows[second, cols], mine[upper, :]) + mm_tn(early_got[second, cols], got[upper, :])
    if whole:
        outs[0][...] = full[...]
        return
    part = half // 2
    send_a, send_b, keep_a, keep_b = outs
    for at, bit, send, keep in ((0, Y, send_a, keep_a), (half, Z0, send_b, keep_b)):
        yours = pl.multiple_of(at + (1 - meta[bit]) * part, part)
        send[...] = full[pl.ds(yours, part), :].astype(BF16)
        keep[...] = full[pl.ds(pl.multiple_of(at + meta[bit] * part, part), part), :]


def slots_kernel(
    chosen_in, attended, rate_in, seen_here, seen_there, moved_here, moved_there, w_router, gain_attn,
    grad_query, grad_key, grad_value, w_query, w_key, w_value, grad_hidden, small,
    update, grad_chosen, vectors,
):
    chosen = chosen_in[...].astype(F32)
    rate = rate_in[:, :1]
    seen = seen_here[...].astype(F32) + seen_there[...].astype(F32)
    delta = attended[...] + (moved_here[...].astype(F32) + moved_there[...].astype(F32))
    update[...] = (rate * delta).astype(BF16)
    score = rate * (1.0 - rate) * jnp.sum(seen * delta, axis=-1, keepdims=True)
    grad_normed = (
        mm_nt(grad_query[...], w_query[...])
        + mm_nt(grad_key[...], w_key[...])
        + mm_nt(grad_value[...], w_value[...])
    )
    back, gain_grad = norm_back(chosen, gain_attn[...], grad_normed)
    grad_chosen[...] = (back + grad_hidden[...] + score * w_router[...].astype(F32)).astype(BF16)
    vectors[...] = small[...]
    vectors[0:1, :] = jnp.sum(score * chosen, axis=0, keepdims=True)
    vectors[1:2, :] = gain_grad


def reduce_kernel(plan, gots, sends, meta, *refs):
    keeps, refs = refs[: len(plan)], refs[len(plan) :]
    got, refs = refs[:gots], refs[gots:]
    send, kept = refs[:sends], refs[sends:]
    for keep, new, (rows, bit, g, g_row, t, t_row) in zip(keeps, kept, plan):
        half = rows // 2
        mine = pl.multiple_of(meta[bit] * half, half)
        yours = pl.multiple_of((1 - meta[bit]) * half, half)
        send[t][t_row : t_row + half, :] = (
            keep[pl.ds(yours, half), :] + got[g][pl.ds(g_row + yours, half), :].astype(F32)
        ).astype(BF16)
        new[...] = keep[pl.ds(mine, half), :] + got[g][pl.ds(g_row + mine, half), :].astype(F32)


def split_vectors(v):
    high = v.astype(BF16).astype(F32)
    return jnp.concatenate([high, (v - high).astype(BF16).astype(F32)], axis=0)


def join_vectors(v):
    return v[:8, :] + v[8:, :]


def reduce_small_kernel(plan, gots, sends, meta, vectors, *refs):
    reduce_kernel(plan, gots, sends, meta, *refs)
    send = refs[len(plan) + gots + sends - 1]
    send[send.shape[0] - 16 :, :] = split_vectors(vectors[...]).astype(BF16)


def round_kernel(keep, got, cur):
    cur[...] = (keep[...] + got[...].astype(F32)).astype(BF16)


def round_both_kernel(vectors, first, second, got_first, got_second, cur, out):
    rows = first.shape[0]
    cur[:rows, :] = (first[...] + got_first[...].astype(F32)).astype(BF16)
    cur[rows : 2 * rows, :] = (second[...] + got_second[:rows, :].astype(F32)).astype(BF16)
    own = join_vectors(split_vectors(vectors[...])) + join_vectors(got_second[rows:, :].astype(F32))
    cur[2 * rows :, :] = split_vectors(own).astype(BF16)
    out[...] = own


def last_kernel(cur, got, out):
    out[...] = (cur[...].astype(F32) + got[...].astype(F32)).astype(BF16)


def last_both_kernel(vectors, cur, got, first, second, both, out):
    rows = second.shape[0]
    for at, piece in ((0, first), (rows, second)):
        piece[:rows, :] = (cur[at : at + rows, :].astype(F32) + got[at : at + rows, :].astype(F32)).astype(BF16)
        both[at : at + rows, :] = piece[:rows, :]
    own = join_vectors(split_vectors(vectors[...])) + join_vectors(got[2 * rows :, :].astype(F32))
    first[rows:, :] = split_vectors(own).astype(BF16)
    out[...] = own


def join_kernel(plan, meta, *refs):
    count = len(plan)
    for (rows, bit, row, got_row), own, got, out in zip(
        plan, refs[:count], refs[count : 2 * count], refs[2 * count :]
    ):
        mine = pl.multiple_of(meta[bit] * rows, rows)
        yours = pl.multiple_of((1 - meta[bit]) * rows, rows)
        out[pl.ds(mine, rows), :] = own[row : row + rows, :].astype(out.dtype)
        out[pl.ds(yours, rows), :] = got[got_row : got_row + rows, :].astype(out.dtype)


def join_both_kernel(meta, vectors, own_a, own_b, got_a, got_b, out_a, out_b, both, far, *sums):
    rows = own_b.shape[0]
    for n, bit, own, got, out in ((0, Z0, own_a, got_a, out_a), (1, Y, own_b, got_b, out_b)):
        mine = pl.multiple_of(meta[bit] * rows, rows)
        yours = pl.multiple_of((1 - meta[bit]) * rows, rows)
        out[pl.ds(mine, rows), :] = own[:rows, :]
        out[pl.ds(yours, rows), :] = got[:rows, :]
        both[2 * n * rows : 2 * (n + 1) * rows, :] = out[...]
        far[n * rows : (n + 1) * rows, :] = got[:rows, :]
    total = join_vectors(split_vectors(vectors[...])) + join_vectors(got_a[rows:, :].astype(F32))
    for n, out in enumerate(sums):
        out[...] = total[n, :]


def stack_kernel(got_a, got_b, late):
    rows = got_a.shape[0]
    late[:rows, :] = got_a[...]
    late[rows:, :] = got_b[...]


def attention_kernel(far, parts, meta, *refs):
    outs, (block, sems) = refs[-6:-2], refs[-2:]
    core, side = meta[1], meta[3] ^ far
    rows = block.shape[1]
    count = sum(n for _, n in parts)
    copies = []
    for other in range(2):
        pieces = list(refs[other * count : (other + 1) * count])
        for late, arrays in parts:
            here, pieces = pieces[:arrays], pieces[arrays:]
            size = rows // arrays
            for packet, bit, inner in ((0, meta[Y], meta[Z0]), (1, meta[Z0], meta[Y])):
                slot = len(copies)
                for n, piece in enumerate(here):
                    at = pl.multiple_of((inner ^ n) * size, 8) if arrays == 2 else 0
                    block[slot, pl.ds(at, size), :] = piece[packet * size : (packet + 1) * size, :].astype(F32)
                at = pl.ds(pl.multiple_of((side * 2 + (bit ^ late)) * rows, 8), rows)
                for m, out in enumerate(outs):

                    @pl.when(2 * (core ^ other) + packet == m)
                    def _():
                        pltpu.make_async_copy(block.at[slot], out.at[at, :], sems.at[slot]).start()

                copies.append(pltpu.make_async_copy(block.at[slot], outs[0].at[at, :], sems.at[slot]))
    for copy in copies:
        copy.wait()


def half_kernel(bit, theirs, meta, piece, *refs):
    out, block, sem = refs[-3:]
    rows = piece.shape[0]
    block[...] = piece[...].astype(F32)
    at = pl.multiple_of((meta[bit] ^ theirs) * rows, rows)
    copy = pltpu.make_async_copy(block, out.at[pl.ds(at, rows), :], sem)
    copy.start()
    copy.wait()


def swap(v, axis, size, bits):
    return lax.ppermute(v, axis, [(i, i ^ bits) for i in range(size)])


def body(
    batch, tokens, lengths, picks, w_router, gain_attn, gain_mlp, w_query, w_key, w_value, w_out,
    w_up, w_down, cotangent,
):
    place, index = lax.axis_index("seq"), lax.axis_index("batch")
    core, side = place % 2, place // 2
    seqs, length, width = tokens.shape
    local = picks.shape[1]
    slots = 4 * local
    n, half = width, width // 2
    hidden_units = w_up.shape[1]
    across = functools.partial(swap, axis="seq", size=4)
    along = lambda v, bit: swap(v, "batch", batch, 1 << bit)
    row = lambda v: v.reshape(1, width)
    gain_attn, gain_mlp, w_router = row(gain_attn), row(gain_mlp), row(w_router)
    meta = jnp.stack(
        [place, core, index, side] + [place ^ k for k in range(4)] + [(index >> k) & 1 for k in range(3)]
    ).astype(jnp.int32)
    rows = lambda count: ((count, width), BF16)
    wide = lambda count: ((count, width), F32)
    hot = ((slots, length), BF16)
    act = ((slots, hidden_units), BF16)
    slope = ((slots, hidden_units), F32)

    got = [across(picks, bits=k) for k in (1, 2, 3)]
    own, other, hot_own, hot_other = call(
        "SE", select_kernel, [meta, *got, picks, tokens], [rows(slots)] * 2 + [hot] * 2,
        specs=[SMEM] + [VMEM] * 3 + [HBM] * 2,
        scratch=[
            pltpu.VMEM((2, length, width), BF16), pltpu.VMEM(picks.shape, jnp.int32),
            pltpu.SemaphoreType.DMA((3,)),
        ],
        vmem=52,
    )
    up_other, down_other = across(w_up, bits=1), across(w_down, bits=1)
    here = own + across(other, bits=1)
    there = across(here, bits=2)
    own, *other = call(
        "SA", select_again_kernel, [meta, hot_own, hot_other, cotangent], [rows(slots)] + [rows(slots // 2)] * 2,
        specs=[SMEM] + [VMEM] * 3,
    )
    seen_here = own + jnp.concatenate([across(v, bits=1) for v in other], axis=0)
    seen_there = across(seen_here, bits=2)

    (
        chosen, normed, query, keys, values, probs, mixed, attended, normed_mlp, rate,
        act_own, act_other, slope_own, slope_other, early_rows, late_rows,
    ) = call(
        "AT", attend_kernel,
        [meta, lengths, here, there, w_router, gain_attn, gain_mlp, w_query, w_key, w_value, w_out, w_up, up_other],
        [rows(slots)] * 5 + [((NH, slots, slots), F32), rows(slots), wide(slots), rows(slots), ((slots, 128), F32)]
        + [act] * 2 + [slope] * 2 + [rows(2 * slots)] * 2,
        specs=[SMEM] * 2 + [VMEM] * 9 + [HBM, VMEM], after=[seen_here],
        scratch=[pltpu.VMEM(w_up.shape, BF16), pltpu.SemaphoreType.DMA],
    )
    early_got, late_got = across(early_rows, bits=1), across(late_rows, bits=1)
    back_own, moved_rows, gn_here = call(
        "ML", mlp_kernel,
        [rate, seen_here, seen_there, slope_own, slope_other, w_up, up_other, w_down, down_other],
        [act, rows(2 * slots), rows(slots)],
    )
    gn_there = across(gn_here, bits=2)
    moved_got = across(moved_rows, bits=1)

    def moved_part(after):
        moved = call("MV", moved_kernel, [act_own, act_other, w_down, down_other], [rows(slots)], after=after)[0]
        return moved, across(moved, bits=2)

    def mlp_grads(outs, after):
        return call(
            "F", functools.partial(mlp_grads_kernel, len(outs) == 2),
            [meta, act_own, back_own, late_rows, moved_rows, late_got, moved_got], outs,
            specs=[SMEM] + [VMEM] * 6, after=after,
        )

    def attend_back(after):
        return call(
            "AB", attend_back_kernel,
            [
                chosen, attended, gain_mlp, gn_here, gn_there, rate, seen_here, seen_there,
                query, keys, values, probs, w_out, meta,
            ],
            [rows(2 * slots)] * 2 + [rows(slots)] * 3 + [wide(slots), wide(8)], specs=[VMEM] * 13 + [SMEM],
            scratch=[pltpu.VMEM((slots, width), BF16)], after=after,
        )

    def attend_grads(mine, got, outs, after):
        return call(
            "FA", functools.partial(attend_grads_kernel, len(outs) == 1),
            [meta, early_rows, early_got, mine, got], outs,
            specs=[SMEM] + [VMEM] * 4, scratch=[pltpu.VMEM((width, width), F32)], after=after,
        )

    def slot_sums(back, moved_here, moved_there, after):
        update, grad_chosen, vectors = call(
            "SL", slots_kernel,
            [
                chosen, attended, rate, seen_here, seen_there, moved_here, moved_there, w_router, gain_attn,
                *back[:3], w_query, w_key, w_value, *back[3:],
            ],
            [rows(slots), rows(slots), wide(8)], after=after,
        )
        return update, grad_chosen, vectors + across(vectors, bits=1)

    def placed(tag, values, mine, core, after=()):
        return call(
            tag, place_kernel, [meta, hot_own, hot_other, values, mine, core],
            [(values.shape, BF16)], specs=[SMEM] + [VMEM] * 5, after=after, token=True,
        )

    if batch != 8:
        whole = ((width, width), F32)
        down, up = mlp_grads([whole] * 2, [])
        mine, theirs, *back = attend_back([])
        update, grad_chosen, vectors = slot_sums(back, *moved_part([]), [])
        attention = attend_grads(mine, across(theirs, bits=1), [whole], [])[0]
        down, up, attention, vectors = lax.psum((down, up, attention, vectors), "batch")
        attention = lax.all_gather(attention, "seq").reshape(2, 2, 2, half, width)
        return (
            placed("P1", tokens, update, across(update, bits=1))[0],
            placed("P2", cotangent, grad_chosen, across(grad_chosen, bits=1))[0],
            vectors[0], vectors[1], vectors[2],
            *(attention[:, m // 2, m % 2].reshape(width, width) for m in range(4)), up, down,
        )

    def reduce(tag, keeps, gots, plan, sends, after=(), vectors=None):
        kernel = functools.partial(reduce_kernel, plan, len(gots), len(sends))
        outs = [rows(count) for count in sends] + [wide(p[0] // 2) for p in plan]
        ins = [meta, *keeps, *gots]
        if vectors is not None:
            kernel = functools.partial(reduce_small_kernel, plan, len(gots), len(sends))
            ins = [meta, vectors, *keeps, *gots]
        return call(tag, kernel, ins, outs, specs=[SMEM] + [VMEM] * (len(ins) - 1), after=after)

    def join(tag, bit, own, got, dtype=BF16, after=(), token=False):
        count = own.shape[0]
        return call(
            tag, functools.partial(join_kernel, [(count, bit, 0, 0)]), [meta, own, got],
            [((2 * count, width), dtype)], specs=[SMEM] + [VMEM] * 2, after=after, token=token,
        )

    def attention(tag, far, parts, pieces, outs=(), after=()):
        return call(
            tag, functools.partial(attention_kernel, far, parts), [meta, *pieces, *outs], [wide(width)] * 4,
            specs=[SMEM] + [VMEM] * len(pieces) + [HBM] * len(outs), out_specs=[HBM] * 4,
            scratch=[pltpu.VMEM((4 * len(parts), half // 2, width), F32), pltpu.SemaphoreType.DMA((4 * len(parts),))],
            aliases={1 + len(pieces) + m: m for m in range(len(outs))}, after=after, token=True, name=tag,
        )

    def write_half(tag, bit, theirs, piece, outs=(), after=()):
        return call(
            tag, functools.partial(half_kernel, bit, theirs), [meta, piece, *outs], [wide(width)],
            specs=[SMEM, VMEM] + [HBM] * len(outs), out_specs=[HBM],
            scratch=[pltpu.VMEM(piece.shape, F32), pltpu.SemaphoreType.DMA],
            aliases={2: 0} if outs else {}, after=after, token=True,
        )

    v, moved = {}, {}

    def kept(name, value):
        moved[name] = value
        return value

    def step_mv(after):
        v["moved"], moved["M"] = moved_part(after)
        return v["moved"]

    def step_f(after):
        d, u, v["d_keep"], v["u_keep"] = mlp_grads([rows(half)] * 2 + [wide(half)] * 2, after)
        v["d"], v["u"] = kept("d1", along(d, 0)), kept("u1", along(u, 1))
        return v["d_keep"]

    def step_ab(after):
        v["mine"], theirs, *v["back"] = attend_back(after)
        v["got"] = kept("th", across(theirs, bits=1))
        return v["back"][-1]

    def step_sl(after):
        v["update"], v["grad_chosen"], v["vectors"] = slot_sums(
            v["back"], v["moved"], moved["M"], after
        )
        v["update_core"] = kept("up", across(v["update"], bits=1))
        v["chosen_core"] = kept("gc", across(v["grad_chosen"], bits=1))
        return v["update"]

    def step_fa(after):
        a, b, v["a_keep"], v["b_keep"] = attend_grads(
            v["mine"], v["got"], [rows(half // 2)] * 2 + [wide(half // 2)] * 2, after
        )
        v["a"], v["b"] = kept("a1", along(a, 0)), kept("b1", along(b, 1))
        return v["a_keep"]

    def step_r2(after):
        send, v["d_keep"] = reduce("R2", [v["d_keep"]], [v["d"]], [(n // 2, Z0, 0, 0, 0, 0)], [n // 4], after)
        v["d"] = kept("d2", along(send, 1))
        return v["d_keep"]

    def step_r2u(after):
        send, v["u_keep"] = reduce("R2U", [v["u_keep"]], [v["u"]], [(n // 2, Y, 0, 0, 0, 0)], [n // 4], after)
        v["u"] = kept("u2", along(send, 0))
        return v["u_keep"]

    def step_a2(after):
        a, b, v["a_keep"], v["b_keep"] = reduce(
            "A2", [v["a_keep"], v["b_keep"]], [v["a"], v["b"]],
            [(half // 2, Z0, 0, 0, 0, 0), (half // 2, Y, 1, 0, 1, 0)],
            [half // 4, half // 4 + 16], after, v["vectors"],
        )
        v["a"], v["b"] = kept("a2", along(a, 1)), kept("b2", along(b, 0))
        return v["a_keep"]

    def third(tag, key):
        def step(after):
            v[key + "_cur"] = call(tag, round_kernel, [v[key + "_keep"], v[key]], [rows(n // 4)], after=after)[0]
            v[key] = kept(key + "3", along(v[key + "_cur"], 2))
            return v[key + "_cur"]

        return step

    def step_a3(after):
        v["ab_cur"], v["vectors"] = call(
            "A3", round_both_kernel, [v["vectors"], v["a_keep"], v["b_keep"], v["a"], v["b"]],
            [rows(half // 2 + 16), wide(8)], after=after,
        )
        v["ab"] = kept("ab3", along(v["ab_cur"], 2))
        return v["vectors"]

    def fourth(tag, key, bit):
        def step(after):
            v[key + "_all"] = call(tag, last_kernel, [v[key + "_cur"], v[key]], [rows(n // 4)], after=after)[0]
            v[key] = kept(key + "5", along(v[key + "_all"], bit))
            return v[key + "_all"]

        return step

    def step_a4(after):
        v["a_all"], v["b_all"], near, v["vectors"] = call(
            "A4", last_both_kernel, [v["vectors"], v["ab_cur"], v["ab"]],
            [rows(half // 4 + 16), rows(half // 4), rows(half // 2), wide(8)], after=after,
        )
        v["a"], v["b"] = kept("a5", along(v["a_all"], 1)), kept("b5", along(v["b_all"], 0))
        v["near"] = kept("x1", across(near, bits=2))
        return v["a_all"]

    def step_a5(after):
        a, b, v["early"], far, *v["vectors"] = call(
            "A5", join_both_kernel, [meta, v["vectors"], v["a_all"], v["b_all"], v["a"], v["b"]],
            [rows(half // 2)] * 2 + [rows(half), rows(half // 2)] + [((width,), F32)] * 3,
            specs=[SMEM] + [VMEM] * 5, after=after,
        )
        v["a"], v["b"] = kept("a6", along(a, 0)), kept("b6", along(b, 1))
        v["far"] = kept("x2", across(far, bits=2))
        v["early_core"] = kept("ce", across(v["early"], bits=1))
        return v["early"]

    def step_a6(after):
        v["late"] = call("A6", stack_kernel, [v["a"], v["b"]], [rows(half)], after=after)[0]
        v["side"] = kept("xl", across(v["late"], bits=2))
        v["late_core"] = kept("cl", across(v["late"], bits=1))
        return v["late"]

    def fifth(tag, key, bit, along_bit):
        def step(after):
            v[key + "_all"] = join(tag, bit, v[key + "_all"], v[key], after=after)[0]
            v[key] = kept(key + "6", along(v[key + "_all"], along_bit))
            return v[key + "_all"]

        return step

    def halves(tag, key, bit, theirs):
        def step(after):
            outs = [v["grad_" + key]] if theirs else []
            piece = v[key] if theirs else v[key + "_all"]
            v["grad_" + key], token = write_half(tag, bit, theirs, piece, outs, after)
            return token

        return step

    def place(tag, name, values, mine, core):
        def step(after):
            v[name], token = placed(tag, values, v[mine], v[core], after)
            return token

        return step

    def step_at0(after):
        pieces = [v["early"], v["late"], v["early_core"], v["late_core"]]
        *v["grads"], token = attention("AT0", 0, ((0, 1), (1, 1)), pieces, after=after)
        return token

    def step_xe(after):
        near, far, *_ = lax.optimization_barrier((v["near"], v["far"], *after))
        v["side_early"] = [near, far, kept("g1", across(near, bits=1)), kept("g2", across(far, bits=1))]
        return after[0]

    def step_ate(after):
        *v["grads"], token = attention("ATE", 1, ((0, 2),), v["side_early"], v["grads"], after)
        return token

    def step_xc(after):
        side, *_ = lax.optimization_barrier((v["side"], *after))
        v["side_late"] = [side, across(side, bits=1)]
        return after[0]

    def step_atl(after):
        *v["grads"], token = attention("ATL", 1, ((1, 1),), v["side_late"], v["grads"], after)
        return token

    steps = dict(
        F=step_f, AB=step_ab, SL=step_sl, FA=step_fa, R2=step_r2, R2U=step_r2u, A2=step_a2, A3=step_a3,
        D3=third("D3", "d"), U3=third("U3", "u"), D4=fourth("D4", "d", 1), U4=fourth("U4", "u", 0), A4=step_a4,
        A5=step_a5, A6=step_a6, D5=fifth("D5", "d", Z0, 0), U5=fifth("U5", "u", Y, 1), DH=halves("DH", "d", Y, 0),
        DU=halves("DU", "d", Y, 1), UH=halves("UH", "u", Z0, 0), UU=halves("UU", "u", Z0, 1), MV=step_mv, XE=step_xe,
        ATE=step_ate, ATL=step_atl, P1=place("P1", "output", tokens, "update", "update_core"),
        P2=place("P2", "grad_tokens", cotangent, "grad_chosen", "chosen_core"), AT0=step_at0, XC=step_xc,
    )
    after = []
    for name in ORDER:
        after = [steps[name](after + [moved[key] for key in HOLD.get(name, ())])]
    return (
        v["output"], v["grad_tokens"], *v["vectors"], *v["grads"], v["grad_u"], v["grad_d"],
    )


def solution(mesh):
    rows, whole = P("batch", "seq", None), P()
    return jax.shard_map(
        functools.partial(body, mesh.shape["batch"]),
        mesh=mesh,
        in_specs=(
            rows, P("batch"), P("batch", "seq"), whole, whole, whole, whole, whole, whole, whole,
            P(None, "seq"), P("seq", None), rows,
        ),
        out_specs=(
            rows, rows, whole, whole, whole, whole, whole, whole, whole,
            P(None, "seq"), P("seq", None),
        ),
        check_vma=False,
    )
```

```python
import functools

import jax
import jax.numpy as jnp
from jax import lax
from jax.experimental import pallas as pl
from jax.experimental.pallas import tpu as pltpu
from jax.sharding import PartitionSpec as P

NH = 12
Y, Z0, Z1 = 8, 9, 10
ORDER = ("F", "MV", "AB", "R2", "FA", "SL", "D3", "A2", "R2U", "A3", "D4", "P2", "A4", "U3", "P1", "A5", "U4", "A6", "D5", "U5", "XE", "MID", "XC", "FIN")
WORK = {"P1": 600, "U5": 8000, "U4": 2000, "D3": 100, "SL": 300, "P2": 100, "R2": 4000, "A6": 2000, "A4": 1000, "A2": 4000, "AT": 600, "R2U": 2000, "ML": 4000, "F": 2000, "A5": 2000, "SE": 8000, "MV": 4000, "SA": 300, "D5": 300, "FA": 300, "FIN": 4000, "D4": 8000, "A3": 100}
HOLD = {"R2": ["u1"], "D5": ["x2"], "R2U": ["gc"], "U4": ["a6", "x1"], "D3": ["a1"], "A4": ["u2"], "A5": ["d5"]}
EPS = 1e-06
F32 = jnp.float32
BF16 = jnp.bfloat16
VMEM = pl.BlockSpec(memory_space=pltpu.VMEM)
SMEM = pl.BlockSpec(memory_space=pltpu.SMEM)
ANY = pl.BlockSpec(memory_space=pl.ANY)
HBM = pl.BlockSpec(memory_space=pltpu.HBM)


def mm(a, b):
    return jnp.dot(a, b, preferred_element_type=F32)


def mm_nt(a, b):
    return lax.dot_general(a, b, (((1,), (1,)), ((), ())), preferred_element_type=F32)


def mm_tn(a, b):
    return lax.dot_general(a, b, (((0,), (0,)), ((), ())), preferred_element_type=F32)


def call(
    tag, kernel, ins, outs, specs=None, scratch=(), vmem=12, after=(), name=None, token=False,
    out_specs=None, aliases=None,
):
    shapes = [jax.ShapeDtypeStruct(shape, dtype) for shape, dtype in outs]
    results = len(shapes)
    out_specs = list(out_specs or [VMEM] * results)
    if token:
        shapes.append(jax.ShapeDtypeStruct((8, 128), F32))
        out_specs.append(VMEM)
    count, extra = len(ins), len(after)

    def run(*refs):
        rest = refs[count + extra :]
        if token:
            rest[results][...] = jnp.zeros((8, 128), F32)
            rest = rest[:results] + rest[results + 1 :]
        kernel(*refs[:count], *rest)

    return pl.pallas_call(
        run,
        out_shape=tuple(shapes),
        in_specs=(specs or [VMEM] * count) + [ANY] * extra,
        out_specs=tuple(out_specs),
        scratch_shapes=list(scratch),
        input_output_aliases=aliases or {},
        name=name or getattr(kernel, "func", kernel).__name__,
        cost_estimate=pl.CostEstimate(flops=1 + WORK.get(tag, 0) * 1_000_000, bytes_accessed=1, transcendentals=0),
        compiler_params=pltpu.CompilerParams(vmem_limit_bytes=vmem * 1024 * 1024),
    )(*ins, *after)


def select_kernel(meta, p0, p1, p2, p3, rows, other, hot_own, hot_other, local_rows, sem):
    core = meta[1]
    copy = pltpu.make_async_copy(rows.at[1 - core], local_rows, sem)
    copy.start()
    length = rows.shape[1]
    local = p1.shape[1]
    base = meta[0] * length
    down = lax.broadcasted_iota(jnp.int32, (local, local), 0)
    along = lax.broadcasted_iota(jnp.int32, (local, local), 1)
    places = lax.broadcasted_iota(jnp.int32, (local, length), 1)
    for seq, hot in ((1 - core, hot_other), (core, hot_own)):
        for k, part in enumerate((p0, p1, p2, p3)):
            at = pl.multiple_of(meta[4 + k] * local, local)
            row = part[pl.ds(seq, 1), :]
            column = jnp.sum(jnp.where(down == along, row, 0), axis=1, keepdims=True)
            hot[pl.ds(at, local), :] = jnp.where(column - base == places, 1.0, 0.0).astype(BF16)
    copy.wait()
    other[...] = mm(hot_other[...], local_rows[...]).astype(BF16)


def select_again_kernel(meta, hot_own, hot_other, rows, more_rows, own, more_own, first, second):
    core = meta[1]
    half = first.shape[0]
    own[...] = mm(hot_own[...], rows[core]).astype(BF16)
    first[...] = mm(hot_other[:half, :], more_rows[1 - core]).astype(BF16)
    second[...] = mm(hot_other[half:, :], more_rows[1 - core]).astype(BF16)
    more_own[...] = mm(hot_own[...], more_rows[core]).astype(BF16)


def place_kernel(meta, hot_own, hot_other, rows, own, other, out):
    core = meta[1]
    for seq, hot, update in ((core, hot_own, own), (1 - core, hot_other, other)):
        out[seq] = (rows[seq].astype(F32) + mm_tn(hot[...], update[...])).astype(BF16)


def attend_kernel(
    meta, lengths, here, there, w_router, gain_attn, gain_mlp, w_query, w_key, w_value, w_out,
    up_own, up_other, chosen_out, normed_out, query_out, key_out, value_out, probs_out, mixed_out, attended_out,
    normed_mlp_out, rate_out, act_own, act_other, slope_own, slope_other, early_rows, late_rows, up_local, sem,
):
    copy = pltpu.make_async_copy(up_own, up_local, sem)
    copy.start()
    count = lengths[meta[1]] // 8
    slots, width = here.shape
    chosen = here[...].astype(F32) + there[...].astype(F32)
    chosen_out[...] = chosen.astype(BF16)
    score = jnp.sum(chosen * w_router[...].astype(F32), axis=-1, keepdims=True)
    rate = jax.nn.sigmoid(score)
    valid = lax.broadcasted_iota(jnp.int32, (slots, 1), 0) < count
    rate_out[...] = jnp.broadcast_to(jnp.where(valid, rate, 0.0), rate_out.shape)
    scale = lax.rsqrt(jnp.mean(chosen * chosen, axis=-1, keepdims=True) + EPS)
    normed = (chosen * scale * gain_attn[...]).astype(BF16)
    normed_out[...] = normed
    query_out[...] = mm(normed, w_query[...]).astype(BF16)
    key_out[...] = mm(normed, w_key[...]).astype(BF16)
    value_out[...] = mm(normed, w_value[...]).astype(BF16)
    head = width // NH
    pair = 2 * head
    i = lax.broadcasted_iota(jnp.int32, (slots, slots), 0)
    j = lax.broadcasted_iota(jnp.int32, (slots, slots), 1)
    allowed = (j <= i) & (j < count)
    first = lax.broadcasted_iota(jnp.int32, (slots, pair), 1) < head
    for p in range(NH // 2):
        cols = slice(p * pair, (p + 1) * pair)
        query = query_out[:, cols]
        keys = key_out[:, cols]
        values = value_out[:, cols]
        halves = []
        for h in range(2):
            mine = first if h == 0 else ~first
            logits = mm_nt(jnp.where(mine, query, jnp.zeros_like(query)), keys) * (head ** -0.5)
            logits = jnp.where(allowed, logits, -1e30)
            expd = jnp.exp(logits - jnp.max(logits, axis=-1, keepdims=True))
            probs = expd / jnp.sum(expd, axis=-1, keepdims=True)
            probs_out[2 * p + h] = probs
            halves.append(mm(probs.astype(BF16), values))
        mixed_out[:, cols] = jnp.where(first, halves[0], halves[1]).astype(BF16)
    attended = mm(mixed_out[...], w_out[...])
    attended_out[...] = attended
    hidden = chosen + attended
    scale = lax.rsqrt(jnp.mean(hidden * hidden, axis=-1, keepdims=True) + EPS)
    normed_mlp = (hidden * scale * gain_mlp[...]).astype(BF16)
    normed_mlp_out[...] = normed_mlp
    for w_up, act, slope in ((up_other, act_other, slope_other), (up_local, act_own, slope_own)):
        if w_up is up_local:
            copy.wait()
        up = mm(normed_mlp, w_up[...])
        square = up * up
        root = 0.7978845608028654
        t = jnp.tanh(root * (up + 0.044715 * (square * up)))
        act[...] = (0.5 * up * (1.0 + t)).astype(BF16)
        slope[...] = 0.5 * (1.0 + t) + (0.5 * root) * up * (1.0 - t * t) * (1.0 + 0.134145 * square)
    early_rows[:slots, :] = normed_out[...]
    early_rows[slots:, :] = mixed_out[...]
    late_rows[:slots, :] = normed_mlp
    late_rows[slots:, :] = act_other[...]


def mlp_kernel(
    rate, here, there, slope_own, slope_other, up_own, up_other, down_own, down_other,
    back_own, rows, grad_normed,
):
    seen = here[...].astype(F32) + there[...].astype(F32)
    moved = (rate[:, :1] * seen).astype(BF16)
    slots = moved.shape[0]
    rows[:slots, :] = moved
    total = None
    for w_up, w_down, slope, own in (
        (up_own, down_own, slope_own, True),
        (up_other, down_other, slope_other, False),
    ):
        grad_up = (mm_nt(moved, w_down[...]) * slope[...]).astype(BF16)
        if own:
            back_own[...] = grad_up
        else:
            rows[slots:, :] = grad_up
        part = mm_nt(grad_up, w_up[...])
        total = part if total is None else total + part
    grad_normed[...] = total.astype(BF16)


def moved_kernel(act_own, act_other, down_own, down_other, moved):
    moved[...] = (mm(act_own[...], down_own[...]) + mm(act_other[...], down_other[...])).astype(BF16)


def mlp_grads_kernel(whole, meta, act, back, late_rows, rows, late_got, got, *outs):
    slots, width = act.shape
    moved, moved_got = rows[:slots, :], got[:slots, :]
    back_got = got[slots:, :]
    if whole:
        outs[0][...] = mm_tn(act[...], moved) + mm_tn(late_got[slots:, :], moved_got)
        outs[1][...] = mm_tn(late_rows[:slots, :], back[...]) + mm_tn(late_got[:slots, :], back_got)
        return
    half = width // 2
    d_send, u_send, d_keep, u_keep = outs
    for bit, send in ((1, True), (0, False)):
        cols = pl.ds(pl.multiple_of((meta[Y] ^ bit) * half, 128), half)
        d = mm_tn(act[:, cols], moved) + mm_tn(late_got[slots:, cols], moved_got)
        cols = pl.ds(pl.multiple_of((meta[Z0] ^ bit) * half, 128), half)
        u = mm_tn(late_rows[:slots, cols], back[...]) + mm_tn(late_got[:slots, cols], back_got)
        if send:
            d_send[...] = d.astype(BF16)
            u_send[...] = u.astype(BF16)
        else:
            d_keep[...] = d
            u_keep[...] = u


def norm_back(values, gain, grad):
    scale = lax.rsqrt(jnp.mean(values * values, axis=-1, keepdims=True) + EPS)
    scaled = grad * gain
    inner = jnp.mean(scaled * values, axis=-1, keepdims=True)
    back = scale * scaled - values * (scale * scale * scale * inner)
    return back, jnp.sum(grad * values * scale, axis=0, keepdims=True)


def attend_back_kernel(
    chosen_in, attended, gain_mlp, gn_here, gn_there, rate, seen_here, seen_there,
    query_in, key_in, value_in, probs_in, w_out, meta,
    kept_rows, sent_rows, grad_query, grad_key, grad_value, hidden_out, small, mixed_back,
):
    small[...] = jnp.zeros_like(small)
    slots, width = chosen_in.shape
    head = width // NH
    pair = 2 * head
    chosen = chosen_in[...].astype(F32)
    grad_normed_mlp = gn_here[...].astype(F32) + gn_there[...].astype(F32)
    grad_hidden, gain_grad = norm_back(chosen + attended[...], gain_mlp[...], grad_normed_mlp)
    small[2:3, :] = gain_grad
    hidden_out[...] = grad_hidden
    seen = seen_here[...].astype(F32) + seen_there[...].astype(F32)
    grad_attended = (rate[:, :1] * seen + grad_hidden).astype(BF16)
    mixed_back[...] = mm_nt(grad_attended, w_out[...]).astype(BF16)
    first = lax.broadcasted_iota(jnp.int32, (slots, pair), 1) < head
    factor = head ** -0.5
    for p in range(NH // 2):
        cols = slice(p * pair, (p + 1) * pair)
        query = query_in[:, cols]
        keys = key_in[:, cols]
        values = value_in[:, cols]
        back = mixed_back[:, cols]
        back_turned, query_turned = back.T, query.T
        for_query, for_key, for_value = [], [], []
        for h in range(2):
            mine = first if h == 0 else ~first
            rows = slice(h * head, (h + 1) * head)
            probs = probs_in[2 * p + h]
            grad_probs = mm_nt(jnp.where(mine, back, jnp.zeros_like(back)), values)
            for_value.append(mm(back_turned[rows, :], probs.astype(BF16)))
            inner = jnp.sum(grad_probs * probs, axis=-1, keepdims=True)
            grad_logits = (probs * (grad_probs - inner)).astype(BF16)
            for_query.append(mm(grad_logits, keys) * factor)
            for_key.append(mm(query_turned[rows, :], grad_logits) * factor)
        grad_query[:, cols] = jnp.where(first, for_query[0], for_query[1]).astype(BF16)
        grad_key[:, cols] = jnp.concatenate(for_key, axis=0).astype(BF16).T
        grad_value[:, cols] = jnp.concatenate(for_value, axis=0).astype(BF16).T
    for core, (low, high) in enumerate(((kept_rows, sent_rows), (sent_rows, kept_rows))):

        @pl.when(meta[1] == core)
        def _():
            low[:slots, :] = grad_query[...]
            low[slots:, :] = grad_key[...]
            high[:slots, :] = grad_value[...]
            high[slots:, :] = grad_attended


def attend_grads_kernel(whole, meta, *refs):
    early_rows, early_got, mine, got, *outs, full = refs
    slots = mine.shape[0] // 2
    half = mine.shape[1] // 2
    cols = pl.ds(pl.multiple_of(meta[3] * half, 128), half)
    lower, upper = pl.ds(0, slots), pl.ds(slots, slots)
    second = pl.ds(pl.multiple_of(meta[1] * slots, slots), slots)
    full[:half, :] = mm_tn(early_rows[lower, cols], mine[lower, :]) + mm_tn(early_got[lower, cols], got[lower, :])
    full[half:, :] = mm_tn(early_rows[second, cols], mine[upper, :]) + mm_tn(early_got[second, cols], got[upper, :])
    if whole:
        outs[0][...] = full[...]
        return
    part = half // 2
    send_a, send_b, keep_a, keep_b = outs
    for at, bit, send, keep in ((0, Y, send_a, keep_a), (half, Z0, send_b, keep_b)):
        yours = pl.multiple_of(at + (1 - meta[bit]) * part, part)
        send[...] = full[pl.ds(yours, part), :].astype(BF16)
        keep[...] = full[pl.ds(pl.multiple_of(at + meta[bit] * part, part), part), :]


def slots_kernel(
    chosen_in, attended, rate_in, seen_here, seen_there, moved_here, moved_there, w_router, gain_attn,
    grad_query, grad_key, grad_value, w_query, w_key, w_value, grad_hidden, small,
    update, grad_chosen, vectors,
):
    chosen = chosen_in[...].astype(F32)
    rate = rate_in[:, :1]
    seen = seen_here[...].astype(F32) + seen_there[...].astype(F32)
    delta = attended[...] + (moved_here[...].astype(F32) + moved_there[...].astype(F32))
    update[...] = (rate * delta).astype(BF16)
    score = rate * (1.0 - rate) * jnp.sum(seen * delta, axis=-1, keepdims=True)
    grad_normed = (
        mm_nt(grad_query[...], w_query[...])
        + mm_nt(grad_key[...], w_key[...])
        + mm_nt(grad_value[...], w_value[...])
    )
    back, gain_grad = norm_back(chosen, gain_attn[...], grad_normed)
    grad_chosen[...] = (back + grad_hidden[...] + score * w_router[...].astype(F32)).astype(BF16)
    vectors[...] = small[...]
    vectors[0:1, :] = jnp.sum(score * chosen, axis=0, keepdims=True)
    vectors[1:2, :] = gain_grad


def reduce_kernel(plan, gots, sends, meta, *refs):
    keeps, refs = refs[: len(plan)], refs[len(plan) :]
    got, refs = refs[:gots], refs[gots:]
    send, kept = refs[:sends], refs[sends:]
    for keep, new, (rows, bit, g, g_row, t, t_row) in zip(keeps, kept, plan):
        half = rows // 2
        mine = pl.multiple_of(meta[bit] * half, half)
        yours = pl.multiple_of((1 - meta[bit]) * half, half)
        send[t][t_row : t_row + half, :] = (
            keep[pl.ds(yours, half), :] + got[g][pl.ds(g_row + yours, half), :].astype(F32)
        ).astype(BF16)
        new[...] = keep[pl.ds(mine, half), :] + got[g][pl.ds(g_row + mine, half), :].astype(F32)


def split_vectors(v):
    high = v.astype(BF16).astype(F32)
    return jnp.concatenate([high, (v - high).astype(BF16).astype(F32)], axis=0)


def join_vectors(v):
    return v[:8, :] + v[8:, :]


def reduce_small_kernel(plan, gots, sends, meta, vectors, *refs):
    reduce_kernel(plan, gots, sends, meta, *refs)
    send = refs[len(plan) + gots + sends - 1]
    send[send.shape[0] - 16 :, :] = split_vectors(vectors[...]).astype(BF16)


def round_kernel(keep, got, cur):
    cur[...] = (keep[...] + got[...].astype(F32)).astype(BF16)


def round_both_kernel(vectors, first, second, got_first, got_second, cur, out):
    rows = first.shape[0]
    cur[:rows, :] = (first[...] + got_first[...].astype(F32)).astype(BF16)
    cur[rows : 2 * rows, :] = (second[...] + got_second[:rows, :].astype(F32)).astype(BF16)
    own = join_vectors(split_vectors(vectors[...])) + join_vectors(got_second[rows:, :].astype(F32))
    cur[2 * rows :, :] = split_vectors(own).astype(BF16)
    out[...] = own


def last_kernel(cur, got, out):
    out[...] = (cur[...].astype(F32) + got[...].astype(F32)).astype(BF16)


def last_both_kernel(vectors, cur, got, first, second, both, out):
    rows = second.shape[0]
    for at, piece in ((0, first), (rows, second)):
        piece[:rows, :] = (cur[at : at + rows, :].astype(F32) + got[at : at + rows, :].astype(F32)).astype(BF16)
        both[at : at + rows, :] = piece[:rows, :]
    own = join_vectors(split_vectors(vectors[...])) + join_vectors(got[2 * rows :, :].astype(F32))
    first[rows:, :] = split_vectors(own).astype(BF16)
    out[...] = own


def join_kernel(plan, meta, *refs):
    count = len(plan)
    for (rows, bit, row, got_row), own, got, out in zip(
        plan, refs[:count], refs[count : 2 * count], refs[2 * count :]
    ):
        mine = pl.multiple_of(meta[bit] * rows, rows)
        yours = pl.multiple_of((1 - meta[bit]) * rows, rows)
        out[pl.ds(mine, rows), :] = own[row : row + rows, :].astype(out.dtype)
        out[pl.ds(yours, rows), :] = got[got_row : got_row + rows, :].astype(out.dtype)


def join_both_kernel(meta, vectors, own_a, own_b, got_a, got_b, out_a, out_b, both, far, *sums):
    rows = own_b.shape[0]
    for n, bit, own, got, out in ((0, Z0, own_a, got_a, out_a), (1, Y, own_b, got_b, out_b)):
        mine = pl.multiple_of(meta[bit] * rows, rows)
        yours = pl.multiple_of((1 - meta[bit]) * rows, rows)
        out[pl.ds(mine, rows), :] = own[:rows, :]
        out[pl.ds(yours, rows), :] = got[:rows, :]
        both[2 * n * rows : 2 * (n + 1) * rows, :] = out[...]
        far[n * rows : (n + 1) * rows, :] = got[:rows, :]
    total = join_vectors(split_vectors(vectors[...])) + join_vectors(got_a[rows:, :].astype(F32))
    for n, out in enumerate(sums):
        out[...] = total[n, :]


def stack_kernel(got_a, got_b, late):
    rows = got_a.shape[0]
    late[:rows, :] = got_a[...]
    late[rows:, :] = got_b[...]


def start_attention(far, parts, meta, refs, outs, block, sems):
    core, side = meta[1], meta[3] ^ far
    rows = block.shape[1]
    count = sum(n for _, n in parts)
    copies = []
    for other in range(2):
        pieces = list(refs[other * count : (other + 1) * count])
        for late, arrays in parts:
            here, pieces = pieces[:arrays], pieces[arrays:]
            size = rows // arrays
            for packet, bit, inner in ((0, meta[Y], meta[Z0]), (1, meta[Z0], meta[Y])):
                slot = len(copies)
                for n, piece in enumerate(here):
                    at = pl.multiple_of((inner ^ n) * size, 8) if arrays == 2 else 0
                    block[slot, pl.ds(at, size), :] = piece[packet * size : (packet + 1) * size, :].astype(F32)
                at = pl.ds(pl.multiple_of((side * 2 + (bit ^ late)) * rows, 8), rows)
                for m, out in enumerate(outs):

                    @pl.when(2 * (core ^ other) + packet == m)
                    def _():
                        pltpu.make_async_copy(block.at[slot], out.at[at, :], sems.at[slot]).start()

                copies.append(pltpu.make_async_copy(block.at[slot], outs[0].at[at, :], sems.at[slot]))
    return copies


def start_halves(theirs, meta, pieces, outs, block, sems):
    copies = []
    for n, (piece, bit) in enumerate(zip(pieces, (Y, Z0))):
        rows = piece.shape[0]
        block[n] = piece[...].astype(F32)
        at = pl.ds(pl.multiple_of((meta[bit] ^ theirs) * rows, rows), rows)
        copies.append(pltpu.make_async_copy(block.at[n], outs[n].at[at, :], sems.at[n]))
        copies[-1].start()
    return copies


def middle_kernel(meta, *refs):
    near, far, halves, outs = refs[:4], refs[4:8], refs[8:10], refs[10:16]
    near_block, near_sems, far_block, far_sems, half_block, half_sems = refs[16:]
    copies = start_halves(0, meta, halves, outs[4:], half_block, half_sems)
    copies += start_attention(0, ((0, 1), (1, 1)), meta, near, outs[:4], near_block, near_sems)
    copies += start_attention(1, ((0, 2),), meta, far, outs[:4], far_block, far_sems)
    for copy in copies:
        copy.wait()


def final_kernel(meta, side, side_core, d_got, u_got, *refs):
    outs, (block, sems, half_block, half_sems) = refs[-10:-4], refs[-4:]
    copies = start_halves(1, meta, (d_got, u_got), outs[4:], half_block, half_sems)
    copies += start_attention(1, ((1, 1),), meta, (side, side_core), outs[:4], block, sems)
    for copy in copies:
        copy.wait()


def swap(v, axis, size, bits):
    return lax.ppermute(v, axis, [(i, i ^ bits) for i in range(size)])


def body(
    batch, tokens, lengths, picks, w_router, gain_attn, gain_mlp, w_query, w_key, w_value, w_out,
    w_up, w_down, cotangent,
):
    place, index = lax.axis_index("seq"), lax.axis_index("batch")
    core, side = place % 2, place // 2
    seqs, length, width = tokens.shape
    local = picks.shape[1]
    slots = 4 * local
    n, half = width, width // 2
    hidden_units = w_up.shape[1]
    across = functools.partial(swap, axis="seq", size=4)
    along = lambda v, bit: swap(v, "batch", batch, 1 << bit)
    row = lambda v: v.reshape(1, width)
    gain_attn, gain_mlp, w_router = row(gain_attn), row(gain_mlp), row(w_router)
    meta = jnp.stack(
        [place, core, index, side] + [place ^ k for k in range(4)] + [(index >> k) & 1 for k in range(3)]
    ).astype(jnp.int32)
    rows = lambda count: ((count, width), BF16)
    wide = lambda count: ((count, width), F32)
    hot = ((slots, length), BF16)
    act = ((slots, hidden_units), BF16)
    slope = ((slots, hidden_units), F32)

    got = [across(picks, bits=k) for k in (1, 2, 3)]
    own_picks = jnp.where(place < 4, picks, 0)
    other, hot_own, hot_other = call(
        "SE", select_kernel, [meta, own_picks, *got, tokens], [rows(slots)] + [hot] * 2,
        specs=[SMEM] + [VMEM] * 4 + [HBM],
        scratch=[pltpu.VMEM((length, width), BF16), pltpu.SemaphoreType.DMA],
        vmem=52,
    )
    up_other, down_other = across(w_up, bits=1), across(w_down, bits=1)
    other = across(other, bits=1)
    own, seen_here, *more = call(
        "SA", select_again_kernel, [meta, hot_own, hot_other, tokens, cotangent],
        [rows(slots)] * 2 + [rows(slots // 2)] * 2, specs=[SMEM] + [VMEM] * 4,
    )
    here = own + other
    there = across(here, bits=2)
    seen_here = seen_here + jnp.concatenate([across(v, bits=1) for v in more], axis=0)
    seen_there = across(seen_here, bits=2)

    (
        chosen, normed, query, keys, values, probs, mixed, attended, normed_mlp, rate,
        act_own, act_other, slope_own, slope_other, early_rows, late_rows,
    ) = call(
        "AT", attend_kernel,
        [meta, lengths, here, there, w_router, gain_attn, gain_mlp, w_query, w_key, w_value, w_out, w_up, up_other],
        [rows(slots)] * 5 + [((NH, slots, slots), F32), rows(slots), wide(slots), rows(slots), ((slots, 128), F32)]
        + [act] * 2 + [slope] * 2 + [rows(2 * slots)] * 2,
        specs=[SMEM] * 2 + [VMEM] * 9 + [HBM, VMEM], after=[seen_here],
        scratch=[pltpu.VMEM(w_up.shape, BF16), pltpu.SemaphoreType.DMA],
    )
    early_got, late_got = across(early_rows, bits=1), across(late_rows, bits=1)
    back_own, moved_rows, gn_here = call(
        "ML", mlp_kernel,
        [rate, seen_here, seen_there, slope_own, slope_other, w_up, up_other, w_down, down_other],
        [act, rows(2 * slots), rows(slots)],
    )
    gn_there = across(gn_here, bits=2)
    moved_got = across(moved_rows, bits=1)

    def moved_part(after):
        moved = call("MV", moved_kernel, [act_own, act_other, w_down, down_other], [rows(slots)], after=after)[0]
        return moved, across(moved, bits=2)

    def mlp_grads(outs, after):
        return call(
            "F", functools.partial(mlp_grads_kernel, len(outs) == 2),
            [meta, act_own, back_own, late_rows, moved_rows, late_got, moved_got], outs,
            specs=[SMEM] + [VMEM] * 6, after=after,
        )

    def attend_back(after):
        return call(
            "AB", attend_back_kernel,
            [
                chosen, attended, gain_mlp, gn_here, gn_there, rate, seen_here, seen_there,
                query, keys, values, probs, w_out, meta,
            ],
            [rows(2 * slots)] * 2 + [rows(slots)] * 3 + [wide(slots), wide(8)], specs=[VMEM] * 13 + [SMEM],
            scratch=[pltpu.VMEM((slots, width), BF16)], after=after,
        )

    def attend_grads(mine, got, outs, after):
        return call(
            "FA", functools.partial(attend_grads_kernel, len(outs) == 1),
            [meta, early_rows, early_got, mine, got], outs,
            specs=[SMEM] + [VMEM] * 4, scratch=[pltpu.VMEM((width, width), F32)], after=after,
        )

    def slot_sums(back, moved_here, moved_there, after):
        update, grad_chosen, vectors = call(
            "SL", slots_kernel,
            [
                chosen, attended, rate, seen_here, seen_there, moved_here, moved_there, w_router, gain_attn,
                *back[:3], w_query, w_key, w_value, *back[3:],
            ],
            [rows(slots), rows(slots), wide(8)], after=after,
        )
        return update, grad_chosen, vectors + across(vectors, bits=1)

    def placed(tag, values, mine, core, after=()):
        return call(
            tag, place_kernel, [meta, hot_own, hot_other, values, mine, core],
            [(values.shape, BF16)], specs=[SMEM] + [VMEM] * 5, after=after, token=True,
        )

    if batch != 8:
        whole = ((width, width), F32)
        down, up = mlp_grads([whole] * 2, [])
        mine, theirs, *back = attend_back([])
        update, grad_chosen, vectors = slot_sums(back, *moved_part([]), [])
        attention = attend_grads(mine, across(theirs, bits=1), [whole], [])[0]
        down, up, attention, vectors = lax.psum((down, up, attention, vectors), "batch")
        attention = lax.all_gather(attention, "seq").reshape(2, 2, 2, half, width)
        return (
            placed("P1", tokens, update, across(update, bits=1))[0],
            placed("P2", cotangent, grad_chosen, across(grad_chosen, bits=1))[0],
            vectors[0], vectors[1], vectors[2],
            *(attention[:, m // 2, m % 2].reshape(width, width) for m in range(4)), up, down,
        )

    def reduce(tag, keeps, gots, plan, sends, after=(), vectors=None):
        kernel = functools.partial(reduce_kernel, plan, len(gots), len(sends))
        outs = [rows(count) for count in sends] + [wide(p[0] // 2) for p in plan]
        ins = [meta, *keeps, *gots]
        if vectors is not None:
            kernel = functools.partial(reduce_small_kernel, plan, len(gots), len(sends))
            ins = [meta, vectors, *keeps, *gots]
        return call(tag, kernel, ins, outs, specs=[SMEM] + [VMEM] * (len(ins) - 1), after=after)

    def join(tag, bit, own, got, dtype=BF16, after=(), token=False):
        count = own.shape[0]
        return call(
            tag, functools.partial(join_kernel, [(count, bit, 0, 0)]), [meta, own, got],
            [((2 * count, width), dtype)], specs=[SMEM] + [VMEM] * 2, after=after, token=token,
        )

    v, moved = {}, {}

    def kept(name, value):
        moved[name] = value
        return value

    def step_mv(after):
        v["moved"], moved["M"] = moved_part(after)
        return v["moved"]

    def step_f(after):
        d, u, v["d_keep"], v["u_keep"] = mlp_grads([rows(half)] * 2 + [wide(half)] * 2, after)
        v["d"], v["u"] = kept("d1", along(d, 0)), kept("u1", along(u, 1))
        return v["d_keep"]

    def step_ab(after):
        v["mine"], theirs, *v["back"] = attend_back(after)
        v["got"] = kept("th", across(theirs, bits=1))
        return v["back"][-1]

    def step_sl(after):
        v["update"], v["grad_chosen"], v["vectors"] = slot_sums(
            v["back"], v["moved"], moved["M"], after
        )
        v["update_core"] = kept("up", across(v["update"], bits=1))
        v["chosen_core"] = kept("gc", across(v["grad_chosen"], bits=1))
        return v["update"]

    def step_fa(after):
        a, b, v["a_keep"], v["b_keep"] = attend_grads(
            v["mine"], v["got"], [rows(half // 2)] * 2 + [wide(half // 2)] * 2, after
        )
        v["a"], v["b"] = kept("a1", along(a, 0)), kept("b1", along(b, 1))
        return v["a_keep"]

    def step_r2(after):
        send, v["d_keep"] = reduce("R2", [v["d_keep"]], [v["d"]], [(n // 2, Z0, 0, 0, 0, 0)], [n // 4], after)
        v["d"] = kept("d2", along(send, 1))
        return v["d_keep"]

    def step_r2u(after):
        send, v["u_keep"] = reduce("R2U", [v["u_keep"]], [v["u"]], [(n // 2, Y, 0, 0, 0, 0)], [n // 4], after)
        v["u"] = kept("u2", along(send, 0))
        return v["u_keep"]

    def step_a2(after):
        a, b, v["a_keep"], v["b_keep"] = reduce(
            "A2", [v["a_keep"], v["b_keep"]], [v["a"], v["b"]],
            [(half // 2, Z0, 0, 0, 0, 0), (half // 2, Y, 1, 0, 1, 0)],
            [half // 4, half // 4 + 16], after, v["vectors"],
        )
        v["a"], v["b"] = kept("a2", along(a, 1)), kept("b2", along(b, 0))
        return v["a_keep"]

    def third(tag, key):
        def step(after):
            v[key + "_cur"] = call(tag, round_kernel, [v[key + "_keep"], v[key]], [rows(n // 4)], after=after)[0]
            v[key] = kept(key + "3", along(v[key + "_cur"], 2))
            return v[key + "_cur"]

        return step

    def step_a3(after):
        v["ab_cur"], v["vectors"] = call(
            "A3", round_both_kernel, [v["vectors"], v["a_keep"], v["b_keep"], v["a"], v["b"]],
            [rows(half // 2 + 16), wide(8)], after=after,
        )
        v["ab"] = kept("ab3", along(v["ab_cur"], 2))
        return v["vectors"]

    def fourth(tag, key, bit):
        def step(after):
            v[key + "_all"] = call(tag, last_kernel, [v[key + "_cur"], v[key]], [rows(n // 4)], after=after)[0]
            v[key] = kept(key + "5", along(v[key + "_all"], bit))
            return v[key + "_all"]

        return step

    def step_a4(after):
        v["a_all"], v["b_all"], near, v["vectors"] = call(
            "A4", last_both_kernel, [v["vectors"], v["ab_cur"], v["ab"]],
            [rows(half // 4 + 16), rows(half // 4), rows(half // 2), wide(8)], after=after,
        )
        v["a"], v["b"] = kept("a5", along(v["a_all"], 1)), kept("b5", along(v["b_all"], 0))
        v["near"] = kept("x1", across(near, bits=2))
        return v["a_all"]

    def step_a5(after):
        a, b, v["early"], far, *v["vectors"] = call(
            "A5", join_both_kernel, [meta, v["vectors"], v["a_all"], v["b_all"], v["a"], v["b"]],
            [rows(half // 2)] * 2 + [rows(half), rows(half // 2)] + [((width,), F32)] * 3,
            specs=[SMEM] + [VMEM] * 5, after=after,
        )
        v["a"], v["b"] = kept("a6", along(a, 0)), kept("b6", along(b, 1))
        v["far"] = kept("x2", across(far, bits=2))
        v["early_core"] = kept("ce", across(v["early"], bits=1))
        return v["early"]

    def step_a6(after):
        v["late"] = call("A6", stack_kernel, [v["a"], v["b"]], [rows(half)], after=after)[0]
        v["side"] = kept("xl", across(v["late"], bits=2))
        v["late_core"] = kept("cl", across(v["late"], bits=1))
        return v["late"]

    def fifth(tag, key, bit, along_bit):
        def step(after):
            v[key + "_all"] = join(tag, bit, v[key + "_all"], v[key], after=after)[0]
            v[key] = kept(key + "6", along(v[key + "_all"], along_bit))
            return v[key + "_all"]

        return step

    def place(tag, name, values, mine, core):
        def step(after):
            v[name], token = placed(tag, values, v[mine], v[core], after)
            return token

        return step

    def step_xe(after):
        near, far, *_ = lax.optimization_barrier((v["near"], v["far"], *after))
        v["side_early"] = [near, far, kept("g1", across(near, bits=1)), kept("g2", across(far, bits=1))]
        return after[0]

    def blocks(parts):
        return [pltpu.VMEM((4 * parts, half // 2, width), F32), pltpu.SemaphoreType.DMA((4 * parts,))]

    half_blocks = [pltpu.VMEM((2, half, width), F32), pltpu.SemaphoreType.DMA((2,))]

    def step_mid(after):
        pieces = [v["early"], v["late"], v["early_core"], v["late_core"], *v["side_early"], v["d_all"], v["u_all"]]
        *v["grads"], token = call(
            "MID", middle_kernel, [meta, *pieces], [wide(width)] * 6, specs=[SMEM] + [VMEM] * 10, out_specs=[HBM] * 6,
            scratch=blocks(2) + blocks(1) + half_blocks, vmem=14, after=after, token=True,
        )
        return token

    def step_xc(after):
        side, *_ = lax.optimization_barrier((v["side"], *after))
        v["side_late"] = [side, across(side, bits=1)]
        return after[0]

    def step_fin(after):
        ins = [meta, *v["side_late"], v["d"], v["u"], *v["grads"]]
        v["grads"] = call(
            "FIN", final_kernel, ins, [wide(width)] * 6, specs=[SMEM] + [VMEM] * 4 + [HBM] * 6, out_specs=[HBM] * 6,
            scratch=blocks(1) + half_blocks, aliases={5 + m: m for m in range(6)}, after=after,
        )

    steps = dict(
        F=step_f, AB=step_ab, SL=step_sl, FA=step_fa, R2=step_r2, R2U=step_r2u, A2=step_a2, A3=step_a3,
        D3=third("D3", "d"), U3=third("U3", "u"), D4=fourth("D4", "d", 1), U4=fourth("U4", "u", 0), A4=step_a4,
        A5=step_a5, A6=step_a6, D5=fifth("D5", "d", Z0, 0), U5=fifth("U5", "u", Y, 1), MV=step_mv, XE=step_xe,
        MID=step_mid, FIN=step_fin, P1=place("P1", "output", tokens, "update", "update_core"),
        P2=place("P2", "grad_tokens", cotangent, "grad_chosen", "chosen_core"), XC=step_xc,
    )
    after = []
    for name in ORDER:
        after = [steps[name](after + [moved[key] for key in HOLD.get(name, ())])]
    return (
        v["output"], v["grad_tokens"], *v["vectors"], *v["grads"][:4], v["grads"][5], v["grads"][4],
    )


def solution(mesh):
    rows, whole = P("batch", "seq", None), P()
    return jax.shard_map(
        functools.partial(body, mesh.shape["batch"]),
        mesh=mesh,
        in_specs=(
            rows, P("batch"), P("batch", "seq"), whole, whole, whole, whole, whole, whole, whole,
            P(None, "seq"), P("seq", None), rows,
        ),
        out_specs=(
            rows, rows, whole, whole, whole, whole, whole, whole, whole,
            P(None, "seq"), P("seq", None),
        ),
        check_vma=False,
    )
```
